32 devices in a mesh: section: 4 (over y, x), fsdp: 8 (over z, core).
Axes of the slice: x: 2, y: 2, z: 4, core: 2. Of those that a mesh axis runs over, the one named last changes fastest.
Arguments:
- saved_inputs: bfloat16 [4, 2, 2048, 2048], P('section', None, 'fsdp'), may hold values from -600 to 600
- saved_queries: bfloat16 [4, 2, 2048, 1024], P('section', None, 'fsdp'), may hold values from -300 to 300
- saved_keys: bfloat16 [4, 2, 2048, 256], P('section', None, 'fsdp'), may hold values from -6 to 6
- saved_values: bfloat16 [4, 2, 2048, 256], P('section', None, 'fsdp'), may hold values from -6 to 6
- cotangent: bfloat16 [2, 2048, 2048], P(None, 'fsdp'), may hold values from -6 to 6
- norm_gain: bfloat16 [4, 2048], P('section'), may hold values from 0.099609375 to 1.8984375
- query_weight: bfloat16 [4, 2048, 1024], P('section', 'fsdp'), may hold values from -0.125 to 0.125
- key_weight: bfloat16 [4, 2048, 256], P('section', 'fsdp'), may hold values from -0.125 to 0.125
- value_weight: bfloat16 [4, 2048, 256], P('section', 'fsdp'), may hold values from -0.125 to 0.125
- output_weight: bfloat16 [4, 2048, 1024], P('section', 'fsdp'), may hold values from -0.1875 to 0.1875
Outputs:
- act_grads: bfloat16 [4, 2, 2048, 2048], P('section', None, 'fsdp')
- grad_query: bfloat16 [4, 2048, 1024], P('section', 'fsdp')
- grad_key: bfloat16 [4, 2048, 256], P('section', 'fsdp')
- grad_value: bfloat16 [4, 2048, 256], P('section', 'fsdp')
- grad_output: bfloat16 [4, 2048, 1024], P('section', 'fsdp')
The draws below stay inside these ranges and needn't reach their ends.
All inputs are finite; a program needn't handle non-finite values.
Results may differ from the reference program's by a relative error of at most 0.024.
Values may be sent and summed in bfloat16 or wider, within the bound.
A program may use at most 128 MiB of HBM per device.

```python
import math
import jax
import jax.numpy as jnp
from jax import lax

D = 2048
HEADS = 16
KVH = 4
HD = 64
SEQ = 256
MICRO = 2
LAYERS = 4
TOKENS = 2048
QD = 1024
KVD = 256
QKV = 1536


def shared_keys(key):
    base = jax.random.normal(jax.random.fold_in(key, 101), (LAYERS, MICRO, TOKENS, KVD), jnp.float32)
    return jnp.clip(base, -6.0, 6.0)


def draw_saved_inputs(key, part):
    key = jax.random.fold_in(key, 7)
    row_key, col_key, noise_key = jax.random.split(key, 3)
    row_scale = jnp.exp(jax.random.uniform(row_key, (LAYERS, MICRO, TOKENS, 1), jnp.float32, 0.0, math.log(10.0)))
    col_scale = jnp.exp(jax.random.uniform(col_key, (LAYERS, 1, 1, D), jnp.float32, 0.0, math.log(10.0)))
    noise = jnp.clip(jax.random.normal(noise_key, (LAYERS, MICRO, TOKENS, D), jnp.float32), -6.0, 6.0)
    return (noise * row_scale * col_scale).astype(jnp.bfloat16)


def draw_saved_keys(key, part):
    base = shared_keys(key)
    return base.astype(jnp.bfloat16)


def draw_saved_queries(key, part):
    key = jax.random.fold_in(key, 5)
    queries = jnp.clip(jax.random.normal(key, (LAYERS, MICRO, TOKENS, QD), jnp.float32), -6.0, 6.0)
    return queries.astype(jnp.bfloat16)


def level_of(key, shape, cuts, smallest, high):
    level = 1.0
    for position, shards_of in cuts:
        steps = jax.random.uniform(jax.random.fold_in(jax.random.fold_in(key, 6), position), (shards_of,), jnp.float32, smallest / len(cuts), high / len(cuts))
        level = level * jnp.repeat(jnp.exp(steps), shape[position] // shards_of).reshape((-1,) + (1,) * (len(shape) - 1 - position))
    return level


def centred(key, shape, scale, most, cuts=(), held_as=jnp.bfloat16):
    level = level_of(key, shape, cuts, -0.22, 0.18) if cuts else 1.0
    values = jax.random.normal(key, shape, jnp.float32) * scale * level
    return jnp.minimum(jnp.maximum(values, -most), most).astype(held_as)


def setup_inputs(seed: int = 0) -> dict:
    splits = jax.random.split(jax.random.key(seed), 11)
    saved_inputs = draw_saved_inputs(jax.random.fold_in(splits[10], 71), 0)
    saved_queries = draw_saved_queries(jax.random.fold_in(splits[10], 71), 0)
    saved_keys = draw_saved_keys(jax.random.fold_in(splits[10], 71), 0)
    saved_values = centred(splits[3], (LAYERS, MICRO, TOKENS, KVD), 1.0, 6.0, ((0, 4), (2, 8)))
    cotangent = centred(splits[4], (MICRO, TOKENS, D), 1.0, 6.0, ((1, 8),))
    norm_gain = jnp.clip(1.0 + 0.18 * jax.random.normal(splits[5], (LAYERS, D), jnp.float32), 0.099609375, 1.8984375).astype(jnp.bfloat16)
    query_weight = centred(splits[6], (LAYERS, D, QD), D ** -0.5, 0.125, ((0, 4), (1, 8)))
    key_weight = centred(splits[7], (LAYERS, D, KVD), D ** -0.5, 0.125, ((0, 4), (1, 8)))
    value_weight = centred(splits[8], (LAYERS, D, KVD), D ** -0.5, 0.125, ((0, 4), (1, 8)))
    output_weight = centred(splits[9], (LAYERS, D, QD), QD ** -0.5, 0.1875, ((0, 4), (1, 8)))
    return {"saved_inputs": saved_inputs, "saved_queries": saved_queries, "saved_keys": saved_keys, "saved_values": saved_values, "cotangent": cotangent, "norm_gain": norm_gain, "query_weight": query_weight, "key_weight": key_weight, "value_weight": value_weight, "output_weight": output_weight}


norm_eps = 1e-05
rotary_base = 500000.0
masked_score = -1e+30

def rotary_tables(length, head_size):
    half_size = head_size // 2
    inverse = jnp.exp(-(2.0 * jnp.arange(half_size, dtype=jnp.float32) / head_size) * math.log(rotary_base))
    angles = jnp.arange(length, dtype=jnp.float32)[:, None] * inverse[None, :]
    return (jnp.cos(angles), jnp.sin(angles))

def rotate_back(grad_rows, cosine_table, sine_table):
    half_size = grad_rows.shape[-1] // 2
    front_half = grad_rows[..., :half_size]
    back_half = grad_rows[..., half_size:]
    cos_rows = cosine_table[:, None, :]
    sin_rows = sine_table[:, None, :]
    return jnp.concatenate([front_half * cos_rows + back_half * sin_rows, back_half * cos_rows - front_half * sin_rows], axis=-1)

def section_backward(inputs, queries, keys, values, upstream, in_full, out_full, gain_row, cosine_table, sine_table):
    sequences = inputs.shape[0] // SEQ
    groups = HEADS // KVH
    scaling = 1.0 / math.sqrt(HD)
    inputs_f = inputs.astype(jnp.float32)
    scale_inv = lax.rsqrt(lax.optimization_barrier(jnp.mean(inputs_f * inputs_f, axis=-1, keepdims=True)) + norm_eps)
    unit_rows = inputs_f * scale_inv
    gain_vec = gain_row.astype(jnp.float32)
    normed = (unit_rows * gain_vec).astype(jnp.bfloat16)
    query_grid = queries.reshape(sequences, SEQ, KVH, groups, HD).astype(jnp.float32)
    key_grid = keys.reshape(sequences, SEQ, KVH, HD).astype(jnp.float32)
    value_grid = values.reshape(sequences, SEQ, KVH, HD).astype(jnp.float32)
    scores = jnp.einsum('ntkgd,nskd->nkgts', query_grid, key_grid) * scaling
    causal = jnp.arange(SEQ)[:, None] >= jnp.arange(SEQ)[None, :]
    scores = jnp.where(causal, scores, masked_score)
    row_peak = lax.optimization_barrier(jnp.max(scores, axis=-1, keepdims=True))
    weights = jnp.exp(scores - row_peak)
    attn_probs = lax.optimization_barrier((weights / lax.optimization_barrier(jnp.sum(weights, axis=-1, keepdims=True))).astype(jnp.bfloat16)).astype(jnp.float32)
    attn_out = jnp.einsum('nkgts,nskd->ntkgd', attn_probs, value_grid).astype(jnp.bfloat16).reshape(-1, QD)
    d_attn = jnp.dot(upstream, out_full, preferred_element_type=jnp.float32).astype(jnp.bfloat16)
    attn_grid = lax.optimization_barrier(d_attn).reshape(sequences, SEQ, KVH, groups, HD).astype(jnp.float32)
    d_probs = jnp.einsum('ntkgd,nskd->nkgts', attn_grid, value_grid)
    row_inner = lax.optimization_barrier(jnp.sum(attn_probs * d_probs, axis=-1, keepdims=True))
    d_scores = lax.optimization_barrier((attn_probs * (d_probs - row_inner) * scaling).astype(jnp.bfloat16)).astype(jnp.float32)
    d_query = jnp.einsum('nkgts,nskd->ntkgd', d_scores, key_grid)
    d_key = jnp.einsum('nkgts,ntkgd->nskd', d_scores, query_grid)
    d_value = jnp.einsum('nkgts,ntkgd->nskd', attn_probs, attn_grid)
    d_query = rotate_back(d_query.reshape(sequences, SEQ, HEADS, HD), cosine_table, sine_table)
    d_key = rotate_back(d_key, cosine_table, sine_table)
    grad_qkv = jnp.concatenate([d_query.reshape(-1, QD), d_key.reshape(-1, KVD), d_value.reshape(-1, KVD)], axis=1).astype(jnp.bfloat16)
    d_normed = jnp.dot(grad_qkv, in_full.T, preferred_element_type=jnp.float32)
    scaled = d_normed * gain_vec
    d_inputs = scale_inv * (scaled - unit_rows * lax.optimization_barrier(jnp.mean(scaled * unit_rows, axis=-1, keepdims=True)))
    grad_in = (upstream.astype(jnp.float32) + d_inputs).astype(jnp.bfloat16)
    return (grad_in, normed, grad_qkv, attn_out)

def per_sequence(stacked):
    micro_count = stacked.shape[0]
    sequences = stacked.shape[1] // SEQ
    return stacked.reshape(micro_count, sequences, SEQ, -1).transpose(1, 0, 2, 3).reshape(sequences, micro_count * SEQ, -1)

def weight_grads(normed_all, qkv_all, attn_all, upstream_all):
    blocks = (per_sequence(normed_all), per_sequence(qkv_all), per_sequence(attn_all), per_sequence(upstream_all))

    def add_block(running, seq_block):
        normed_rows, qkv_rows, attn_rows, upstream_rows = seq_block
        in_term = jnp.dot(normed_rows.T, qkv_rows, preferred_element_type=jnp.float32)
        out_term = jnp.dot(upstream_rows.T, attn_rows, preferred_element_type=jnp.float32)
        rounded = lax.optimization_barrier(jnp.concatenate([in_term, out_term], axis=1).astype(jnp.bfloat16))
        return (running + rounded.astype(jnp.float32), None)
    initial = jnp.zeros((D, QKV + QD), jnp.float32)
    running, leftover = lax.scan(add_block, initial, blocks)
    return running.astype(jnp.bfloat16)

def reference(saved_inputs, saved_queries, saved_keys, saved_values, cotangent, norm_gain, query_weight, key_weight, value_weight, output_weight):
    cosine_table, sine_table = rotary_tables(SEQ, HD)
    upstream = [cotangent[micro_index] for micro_index in range(MICRO)]
    act_layers = [None] * LAYERS
    query_layers = [None] * LAYERS
    key_layers = [None] * LAYERS
    value_layers = [None] * LAYERS
    output_layers = [None] * LAYERS
    for layer_index in range(LAYERS - 1, -1, -1):
        in_full = jnp.concatenate([query_weight[layer_index], key_weight[layer_index], value_weight[layer_index]], axis=1)
        results = [section_backward(saved_inputs[layer_index, micro_index], saved_queries[layer_index, micro_index], saved_keys[layer_index, micro_index], saved_values[layer_index, micro_index], upstream[micro_index], in_full, output_weight[layer_index], norm_gain[layer_index], cosine_table, sine_table) for micro_index in range(MICRO)]
        act_layers[layer_index] = jnp.stack([result[0] for result in results])
        summed = weight_grads(jnp.stack([result[1] for result in results]), jnp.stack([result[2] for result in results]), jnp.stack([result[3] for result in results]), jnp.stack(upstream))
        query_layers[layer_index] = summed[:, :QD]
        key_layers[layer_index] = summed[:, QD:QD + KVD]
        value_layers[layer_index] = summed[:, QD + KVD:QKV]
        output_layers[layer_index] = summed[:, QKV:]
        upstream = [result[0] for result in results]
    return (jnp.stack(act_layers), jnp.stack(query_layers), jnp.stack(key_layers), jnp.stack(value_layers), jnp.stack(output_layers))
```

```python
import math

import jax
import jax.numpy as jnp
from jax import lax
from jax.experimental import pallas as pl
from jax.experimental.pallas import tpu as pltpu
from jax.sharding import PartitionSpec as P

HEADS = 16
KVH = 4
HD = 64


norm_eps = 1e-05
rotary_base = 500000.0
masked_score = -1e30


def rotary_tables(length, head_size):
    half_size = head_size // 2
    inverse = jnp.exp(
        -(2.0 * jnp.arange(half_size, dtype=jnp.float32) / head_size) * math.log(rotary_base)
    )
    angles = jnp.arange(length, dtype=jnp.float32)[:, None] * inverse[None, :]
    return (jnp.cos(angles), jnp.sin(angles))


def norm_parts(inputs):
    inputs_f = inputs.astype(jnp.float32)
    scale_inv = lax.rsqrt(jnp.mean(inputs_f * inputs_f, axis=-1, keepdims=True) + norm_eps)
    return (inputs_f * scale_inv, scale_inv)


def forward_parts(inputs, queries, keys, values, gain_row):
    length = inputs.shape[0]
    groups = HEADS // KVH
    unit_rows, scale_inv = norm_parts(inputs)
    normed = (unit_rows * gain_row.astype(jnp.float32)).astype(jnp.bfloat16)
    query_grid = queries.reshape(length, KVH, groups, HD)
    key_grid = keys.reshape(length, KVH, HD)
    value_grid = values.reshape(length, KVH, HD)
    scores = jnp.einsum(
        "tkgd,skd->kgts", query_grid, key_grid, preferred_element_type=jnp.float32
    ) * (1.0 / math.sqrt(HD))
    causal = jnp.arange(length)[:, None] >= jnp.arange(length)[None, :]
    scores = jnp.where(causal, scores, masked_score)
    row_peak = jnp.max(scores, axis=-1, keepdims=True)
    weights = jnp.exp(scores - row_peak)
    attn_probs = (weights / jnp.sum(weights, axis=-1, keepdims=True)).astype(jnp.bfloat16)
    attn_out = jnp.einsum(
        "kgts,skd->tkgd", attn_probs, value_grid, preferred_element_type=jnp.float32
    )
    return (attn_probs, normed, attn_out.astype(jnp.bfloat16).reshape(length, -1))


def chain_kernel(
    cotangent_ref,
    out_full_ref,
    in_full_ref,
    probs_ref,
    keys_ref,
    values_ref,
    queries_ref,
    inputs_ref,
    scale_ref,
    gain_ref,
    table_ref,
    grad_ref,
    qkv_ref,
    upstream_ref,
    held,
    d_attn,
    scaled_rows,
    key_sums,
    value_sums,
    send_sem,
    recv_sem,
    local_sem,
):
    section = lax.axis_index("section")
    sections = lax.axis_size("section")
    is_last = section == sections - 1
    below = lax.rem(section + sections - 1, sections)
    above = lax.rem(section + 1, sections)
    micro_count, length, width = grad_ref.shape
    half_rows = length // 2
    shards = in_full_ref.shape[0]
    shard = in_full_ref.shape[2]
    groups = HEADS // KVH
    qd = HEADS * HD
    kvd = KVH * HD

    barrier = pltpu.get_barrier_semaphore()

    @pl.when(section < sections - 1)
    def _():
        pl.semaphore_signal(
            barrier, inc=1, device_id={"section": above}, device_id_type=pl.DeviceIdType.MESH
        )

    @pl.when(is_last)
    def _():
        own = pltpu.make_async_copy(cotangent_ref, held, local_sem)
        own.start()
        own.wait()

    @pl.when(section > 0)
    def _():
        pl.semaphore_wait(barrier, 1)

    def hop(micro, half):
        rows = pl.ds(half * half_rows, half_rows)
        return pltpu.make_async_remote_copy(
            src_ref=grad_ref.at[micro, rows],
            dst_ref=held.at[micro, rows],
            send_sem=send_sem.at[micro, half],
            recv_sem=recv_sem.at[micro, half],
            device_id={"section": below},
            device_id_type=pl.DeviceIdType.MESH,
        )

    front = lax.broadcasted_iota(jnp.int32, (half_rows, 2 * HD), 1) < HD
    front_ones = jnp.where(front, 1.0, 0.0).astype(jnp.bfloat16)
    back_ones = jnp.where(front, 0.0, 1.0).astype(jnp.bfloat16)

    def both_halves(block):
        return block + pltpu.roll(block, HD, 1)

    def one_micro(micro, carry):
        for half in (1, 0):
            rows = pl.ds(half * half_rows, half_rows)
            span = (half + 1) * half_rows

            @pl.when(section < sections - 1)
            def _():
                hop(micro, half).wait_recv()

            def attn_tile(tile, carry):
                columns = pl.ds(pl.multiple_of(tile * 256, 256), 256)
                d_attn[:, columns] = jnp.dot(
                    held[micro, rows, :],
                    out_full_ref[:, columns],
                    preferred_element_type=jnp.float32,
                ).astype(jnp.bfloat16)
                return carry

            lax.fori_loop(0, qd // 256, attn_tile, 0)
            table = table_ref[rows, :]
            kept = []
            for head in range(KVH):
                pairs = [
                    d_attn[:, (head * groups + 2 * i) * HD : (head * groups + 2 * i + 2) * HD]
                    for i in range(groups // 2)
                ]
                d_rows = jnp.concatenate(
                    [pair * ones for pair in pairs for ones in (front_ones, back_ones)], axis=0
                )
                probs = probs_ref[micro, head, :, rows, :span].reshape(groups * half_rows, span)
                d_probs = jnp.dot(
                    d_rows, values_ref[micro, head, :, :span], preferred_element_type=jnp.float32
                )
                probs_f = probs.astype(jnp.float32)
                row_inner = jnp.sum(probs_f * d_probs, axis=-1, keepdims=True)
                d_scores = (probs_f * (d_probs - row_inner)).astype(jnp.bfloat16)
                d_query = jnp.dot(
                    d_scores, keys_ref[micro, head, :span, :], preferred_element_type=jnp.float32
                )
                turned = [
                    both_halves(d_query[g * half_rows : (g + 1) * half_rows] * table)
                    for g in range(groups)
                ]
                for i in range(groups // 2):
                    start = (head * groups + 2 * i) * HD
                    qkv_ref[micro, rows, start : start + 2 * HD] = jnp.where(
                        front, turned[2 * i], turned[2 * i + 1]
                    ).astype(jnp.bfloat16)
                query_rows = queries_ref[micro, head, :, rows, :].reshape(
                    groups * half_rows, 2 * HD
                )
                across = (((0,), (0,)), ((), ()))
                d_key = lax.dot_general(
                    d_scores, query_rows, across, preferred_element_type=jnp.float32
                )
                d_value = lax.dot_general(
                    probs, d_rows, across, preferred_element_type=jnp.float32
                )
                if half == 1:
                    key_sums[head] = d_key[:half_rows]
                    value_sums[head] = d_value[:half_rows]
                    d_key = d_key[half_rows:]
                    d_value = d_value[half_rows:]
                else:
                    d_key = d_key + key_sums[head]
                    d_value = d_value + value_sums[head]
                kept.append((both_halves(d_key * table), both_halves(d_value)))
                if head % 2 == 1:
                    start = qd + (head - 1) * HD
                    for which in range(2):
                        at = start + which * kvd
                        qkv_ref[micro, rows, at : at + 2 * HD] = jnp.where(
                            front, kept[head - 1][which], kept[head][which]
                        ).astype(jnp.bfloat16)

            scale = scale_ref[micro, rows, :]

            def normed_tile(tile, inner):
                columns = pl.ds(pl.multiple_of(tile * shard, shard), shard)
                d_normed = jnp.dot(
                    qkv_ref[micro, rows, :], in_full_ref[tile], preferred_element_type=jnp.float32
                )
                scaled = d_normed * gain_ref[:, columns].astype(jnp.float32)
                scaled_rows[:, columns] = scaled
                unit = inputs_ref[micro, rows, columns].astype(jnp.float32) * scale
                return inner + jnp.sum(scaled * unit, axis=-1, keepdims=True)

            inner = lax.fori_loop(
                0, shards, normed_tile, jnp.zeros((half_rows, 1), jnp.float32)
            ) * (1.0 / width)

            def grad_tile(tile, carry):
                columns = pl.ds(pl.multiple_of(tile * shard, shard), shard)
                unit = inputs_ref[micro, rows, columns].astype(jnp.float32) * scale
                d_inputs = scale * (scaled_rows[:, columns] - unit * inner)
                grad_ref[micro, rows, columns] = (
                    held[micro, rows, columns].astype(jnp.float32) + d_inputs
                ).astype(jnp.bfloat16)
                return carry

            lax.fori_loop(0, shards, grad_tile, 0)

            @pl.when(section > 0)
            def _():
                hop(micro, half).start()

        return carry

    lax.fori_loop(0, micro_count, one_micro, 0)
    keep = pltpu.make_async_copy(held, upstream_ref, local_sem)
    keep.start()
    keep.wait()

    @pl.when(section > 0)
    def _():
        for micro in range(micro_count):
            for half in (1, 0):
                hop(micro, half).wait_send()


def chain(cotangent, out_full, in_full, probs, keys, values, queries, inputs, scale, gain, table):
    micro_count, length, width = inputs.shape
    half_rows = length // 2
    qd = HEADS * HD
    qkv_width = in_full.shape[1]
    vmem = pl.BlockSpec(memory_space=pltpu.VMEM)
    hbm = pl.BlockSpec(memory_space=pl.ANY)
    return pl.pallas_call(
        chain_kernel,
        out_shape=(
            jax.ShapeDtypeStruct((micro_count, length, width), jnp.bfloat16),
            jax.ShapeDtypeStruct((micro_count, length, qkv_width), jnp.bfloat16),
            jax.ShapeDtypeStruct((micro_count, length, width), jnp.bfloat16),
        ),
        in_specs=[hbm] + [vmem] * 10,
        out_specs=(vmem, vmem, hbm),
        scratch_shapes=[
            pltpu.VMEM((micro_count, length, width), jnp.bfloat16),
            pltpu.VMEM((half_rows, qd), jnp.bfloat16),
            pltpu.VMEM((half_rows, width), jnp.float32),
            pltpu.VMEM((KVH, half_rows, 2 * HD), jnp.float32),
            pltpu.VMEM((KVH, half_rows, 2 * HD), jnp.float32),
            pltpu.SemaphoreType.DMA((micro_count, 2)),
            pltpu.SemaphoreType.DMA((micro_count, 2)),
            pltpu.SemaphoreType.DMA,
        ],
        compiler_params=pltpu.CompilerParams(
            collective_id=0, has_side_effects=True, vmem_limit_bytes=52 * 2**20
        ),
        cost_estimate=pl.CostEstimate(
            flops=2 * micro_count * length * width * (qkv_width + qd),
            bytes_accessed=24 * 2**20,
            transcendentals=0,
        ),
    )(cotangent, out_full, in_full, probs, keys, values, queries, inputs, scale, gain, table)


def with_swapped(rows):
    half_size = HD // 2
    swapped = jnp.concatenate([rows[..., half_size:], rows[..., :half_size]], axis=-1)
    return jnp.concatenate([rows, swapped], axis=-1)


def on_device(
    saved_inputs,
    saved_queries,
    saved_keys,
    saved_values,
    cotangent,
    norm_gain,
    query_weight,
    key_weight,
    value_weight,
    output_weight,
):
    inputs = saved_inputs[0]
    queries = saved_queries[0]
    keys_all = saved_keys[0]
    values_all = saved_values[0]
    gain_row = norm_gain[0]
    micro_count = inputs.shape[0]
    length = inputs.shape[1]
    width = inputs.shape[2]
    groups = HEADS // KVH
    out_full = lax.all_gather(output_weight[0], "fsdp", axis=0, tiled=True)
    in_shard = jnp.concatenate([query_weight[0], key_weight[0], value_weight[0]], axis=1)
    in_full = lax.all_gather(in_shard.T, "fsdp", axis=0, tiled=False)
    qkv_width = in_shard.shape[1]
    forward_all = jax.vmap(forward_parts, in_axes=(0, 0, 0, 0, None))
    attn_probs, normed, attn_out = forward_all(inputs, queries, keys_all, values_all, gain_row)
    scale_inv = norm_parts(inputs)[1]
    cosine, sine = rotary_tables(length, HD)
    table = jnp.concatenate([cosine, cosine, sine, -sine], axis=1)
    query_grid = with_swapped(
        queries.reshape(micro_count, length, KVH, groups, HD).transpose(0, 2, 3, 1, 4)
    )
    key_grid = with_swapped(keys_all.reshape(micro_count, length, KVH, HD).transpose(0, 2, 1, 3))
    value_grid = values_all.reshape(micro_count, length, KVH, HD).transpose(0, 2, 3, 1)
    value_grid = value_grid * jnp.bfloat16(1.0 / math.sqrt(HD))
    value_grid = jnp.concatenate([value_grid, value_grid], axis=2)
    grads, qkv_all, upstream_all = chain(
        cotangent,
        out_full,
        in_full,
        attn_probs,
        key_grid,
        value_grid,
        query_grid,
        inputs,
        scale_inv,
        norm_gain,
        table,
    )
    normed_flat = normed.reshape(micro_count * length, width)
    qkv_flat = qkv_all.reshape(micro_count * length, qkv_width)
    attn_flat = attn_out.reshape(micro_count * length, -1)
    upstream_flat = upstream_all.reshape(micro_count * length, width)
    summed = lax.psum_scatter(
        jnp.concatenate(
            [
                lax.dot_general(
                    normed_flat,
                    qkv_flat,
                    (((0,), (0,)), ((), ())),
                    preferred_element_type=jnp.float32,
                ),
                lax.dot_general(
                    upstream_flat,
                    attn_flat,
                    (((0,), (0,)), ((), ())),
                    preferred_element_type=jnp.float32,
                ),
            ],
            axis=1,
        ).astype(jnp.bfloat16),
        "fsdp",
        scatter_dimension=0,
        tiled=True,
    )
    query_cols = query_weight.shape[2]
    key_cols = key_weight.shape[2]
    grad_query = summed[:, :query_cols]
    grad_key = summed[:, query_cols : query_cols + key_cols]
    grad_value = summed[:, query_cols + key_cols : qkv_width]
    grad_output = summed[:, qkv_width:]
    return (
        grads[None],
        grad_query[None],
        grad_key[None],
        grad_value[None],
        grad_output[None],
    )


def solution(mesh):
    return jax.shard_map(
        on_device,
        mesh=mesh,
        in_specs=(
            P("section", None, "fsdp", None),
            P("section", None, "fsdp", None),
            P("section", None, "fsdp", None),
            P("section", None, "fsdp", None),
            P(None, "fsdp", None),
            P("section", None),
            P("section", "fsdp", None),
            P("section", "fsdp", None),
            P("section", "fsdp", None),
            P("section", "fsdp", None),
        ),
        out_specs=(
            P("section", None, "fsdp", None),
            P("section", "fsdp", None),
            P("section", "fsdp", None),
            P("section", "fsdp", None),
            P("section", "fsdp", None),
        ),
        check_vma=False,
    )
```

```python
import math

import jax
import jax.numpy as jnp
from jax import lax
from jax.experimental import pallas as pl
from jax.experimental.pallas import tpu as pltpu
from jax.sharding import PartitionSpec as P

HEADS = 16
KVH = 4
HD = 64


norm_eps = 1e-05
rotary_base = 500000.0
masked_score = -1e30


def rotary_tables(length, head_size):
    half_size = head_size // 2
    inverse = jnp.exp(
        -(2.0 * jnp.arange(half_size, dtype=jnp.float32) / head_size) * math.log(rotary_base)
    )
    angles = jnp.arange(length, dtype=jnp.float32)[:, None] * inverse[None, :]
    return (jnp.cos(angles), jnp.sin(angles))


def norm_parts(inputs):
    inputs_f = inputs.astype(jnp.float32)
    scale_inv = lax.rsqrt(jnp.mean(inputs_f * inputs_f, axis=-1, keepdims=True) + norm_eps)
    return (inputs_f * scale_inv, scale_inv)


def forward_parts(inputs, queries, keys, values, gain_row):
    length = inputs.shape[0]
    groups = HEADS // KVH
    unit_rows, scale_inv = norm_parts(inputs)
    normed = (unit_rows * gain_row.astype(jnp.float32)).astype(jnp.bfloat16)
    query_grid = queries.reshape(length, KVH, groups, HD)
    key_grid = keys.reshape(length, KVH, HD)
    value_grid = values.reshape(length, KVH, HD)
    scores = jnp.einsum(
        "tkgd,skd->kgts", query_grid, key_grid, preferred_element_type=jnp.float32
    ) * (1.0 / math.sqrt(HD))
    causal = jnp.arange(length)[:, None] >= jnp.arange(length)[None, :]
    scores = jnp.where(causal, scores, masked_score)
    row_peak = jnp.max(scores, axis=-1, keepdims=True)
    weights = jnp.exp(scores - row_peak)
    attn_probs = (weights / jnp.sum(weights, axis=-1, keepdims=True)).astype(jnp.bfloat16)
    attn_out = jnp.einsum(
        "kgts,skd->tkgd", attn_probs, value_grid, preferred_element_type=jnp.float32
    )
    return (attn_probs, normed, attn_out.astype(jnp.bfloat16).reshape(length, -1))


def chain_kernel(
    cotangent_ref,
    out_full_ref,
    in_full_ref,
    probs_ref,
    keys_ref,
    values_ref,
    queries_ref,
    inputs_ref,
    scale_ref,
    gain_ref,
    table_ref,
    grad_ref,
    qkv_ref,
    upstream_ref,
    held,
    d_attn,
    scaled_rows,
    key_sums,
    value_sums,
    send_sem,
    recv_sem,
    local_sem,
):
    section = lax.axis_index("section")
    sections = lax.axis_size("section")
    is_last = section == sections - 1
    below = lax.rem(section + sections - 1, sections)
    above = lax.rem(section + 1, sections)
    micro_count, length, width = grad_ref.shape
    half_rows = length // 2
    shards = in_full_ref.shape[0]
    shard = in_full_ref.shape[2]
    groups = HEADS // KVH
    qd = HEADS * HD
    kvd = KVH * HD

    barrier = pltpu.get_barrier_semaphore()

    @pl.when(section < sections - 1)
    def _():
        pl.semaphore_signal(
            barrier, inc=1, device_id={"section": above}, device_id_type=pl.DeviceIdType.MESH
        )

    @pl.when(is_last)
    def _():
        own = pltpu.make_async_copy(cotangent_ref, held, local_sem)
        own.start()
        own.wait()

    @pl.when(section > 0)
    def _():
        pl.semaphore_wait(barrier, 1)

    def hop(micro, half):
        rows = pl.ds(half * half_rows, half_rows)
        return pltpu.make_async_remote_copy(
            src_ref=grad_ref.at[micro, rows],
            dst_ref=held.at[micro, rows],
            send_sem=send_sem.at[micro, half],
            recv_sem=recv_sem.at[micro, half],
            device_id={"section": below},
            device_id_type=pl.DeviceIdType.MESH,
        )

    front = lax.broadcasted_iota(jnp.int32, (half_rows, 2 * HD), 1) < HD
    front_ones = jnp.where(front, 1.0, 0.0).astype(jnp.bfloat16)
    back_ones = jnp.where(front, 0.0, 1.0).astype(jnp.bfloat16)

    def both_halves(block):
        return block + pltpu.roll(block, HD, 1)

    def one_micro(micro, carry):
        for half in (1, 0):
            rows = pl.ds(half * half_rows, half_rows)
            span = (half + 1) * half_rows

            @pl.when(section < sections - 1)
            def _():
                hop(micro, half).wait_recv()

            def attn_tile(tile, carry):
                columns = pl.ds(pl.multiple_of(tile * 256, 256), 256)
                d_attn[:, columns] = jnp.dot(
                    held[micro, rows, :],
                    out_full_ref[:, columns],
                    preferred_element_type=jnp.float32,
                ).astype(jnp.bfloat16)
                return carry

            lax.fori_loop(0, qd // 256, attn_tile, 0)
            table = table_ref[rows, :]
            kept = []
            for head in range(KVH):
                pairs = [
                    d_attn[:, (head * groups + 2 * i) * HD : (head * groups + 2 * i + 2) * HD]
                    for i in range(groups // 2)
                ]
                d_rows = jnp.concatenate(
                    [pair * ones for pair in pairs for ones in (front_ones, back_ones)], axis=0
                )
                probs = probs_ref[micro, head, :, rows, :span].reshape(groups * half_rows, span)
                d_probs = jnp.dot(
                    d_rows, values_ref[micro, head, :, :span], preferred_element_type=jnp.float32
                )
                probs_f = probs.astype(jnp.float32)
                row_inner = jnp.sum(probs_f * d_probs, axis=-1, keepdims=True)
                d_scores = (probs_f * (d_probs - row_inner)).astype(jnp.bfloat16)
                d_query = jnp.dot(
                    d_scores, keys_ref[micro, head, :span, :], preferred_element_type=jnp.float32
                )
                turned = [
                    both_halves(d_query[g * half_rows : (g + 1) * half_rows] * table)
                    for g in range(groups)
                ]
                for i in range(groups // 2):
                    start = (head * groups + 2 * i) * HD
                    qkv_ref[micro, rows, start : start + 2 * HD] = jnp.where(
                        front, turned[2 * i], turned[2 * i + 1]
                    ).astype(jnp.bfloat16)
                query_rows = queries_ref[micro, head, :, rows, :].reshape(
                    groups * half_rows, 2 * HD
                )
                across = (((0,), (0,)), ((), ()))
                d_key = lax.dot_general(
                    d_scores, query_rows, across, preferred_element_type=jnp.float32
                )
                d_value = lax.dot_general(
                    probs, d_rows, across, preferred_element_type=jnp.float32
                )
                if half == 1:
                    key_sums[head] = d_key[:half_rows]
                    value_sums[head] = d_value[:half_rows]
                    d_key = d_key[half_rows:]
                    d_value = d_value[half_rows:]
                else:
                    d_key = d_key + key_sums[head]
                    d_value = d_value + value_sums[head]
                kept.append((both_halves(d_key * table), both_halves(d_value)))
                if head % 2 == 1:
                    start = qd + (head - 1) * HD
                    for which in range(2):
                        at = start + which * kvd
                        qkv_ref[micro, rows, at : at + 2 * HD] = jnp.where(
                            front, kept[head - 1][which], kept[head][which]
                        ).astype(jnp.bfloat16)

            scale = scale_ref[micro, rows, :]

            def normed_tile(tile, inner):
                columns = pl.ds(pl.multiple_of(tile * shard, shard), shard)
                d_normed = jnp.dot(
                    qkv_ref[micro, rows, :], in_full_ref[tile], preferred_element_type=jnp.float32
                )
                scaled = d_normed * gain_ref[:, columns].astype(jnp.float32)
                scaled_rows[:, columns] = scaled
                unit = inputs_ref[micro, rows, columns].astype(jnp.float32) * scale
                return inner + jnp.sum(scaled * unit, axis=-1, keepdims=True)

            inner = lax.fori_loop(
                0, shards, normed_tile, jnp.zeros((half_rows, 1), jnp.float32)
            ) * (1.0 / width)

            def grad_tile(tile, carry):
                columns = pl.ds(pl.multiple_of(tile * shard, shard), shard)
                unit = inputs_ref[micro, rows, columns].astype(jnp.float32) * scale
                d_inputs = scale * (scaled_rows[:, columns] - unit * inner)
                grad_ref[micro, rows, columns] = (
                    held[micro, rows, columns].astype(jnp.float32) + d_inputs
                ).astype(jnp.bfloat16)
                return carry

            lax.fori_loop(0, shards, grad_tile, 0)

            @pl.when(section > 0)
            def _():
                hop(micro, half).start()

        return carry

    lax.fori_loop(0, micro_count, one_micro, 0)
    keep = pltpu.make_async_copy(held, upstream_ref, local_sem)
    keep.start()
    keep.wait()

    @pl.when(section > 0)
    def _():
        for micro in range(micro_count):
            for half in (1, 0):
                hop(micro, half).wait_send()


def chain(cotangent, out_full, in_full, probs, keys, values, queries, inputs, scale, gain, table):
    micro_count, length, width = inputs.shape
    half_rows = length // 2
    qd = HEADS * HD
    qkv_width = in_full.shape[1]
    vmem = pl.BlockSpec(memory_space=pltpu.VMEM)
    hbm = pl.BlockSpec(memory_space=pl.ANY)
    return pl.pallas_call(
        chain_kernel,
        out_shape=(
            jax.ShapeDtypeStruct((micro_count, length, width), jnp.bfloat16),
            jax.ShapeDtypeStruct((micro_count, length, qkv_width), jnp.bfloat16),
            jax.ShapeDtypeStruct((micro_count, length, width), jnp.bfloat16),
        ),
        in_specs=[hbm] + [vmem] * 10,
        out_specs=(vmem, vmem, hbm),
        scratch_shapes=[
            pltpu.VMEM((micro_count, length, width), jnp.bfloat16),
            pltpu.VMEM((half_rows, qd), jnp.bfloat16),
            pltpu.VMEM((half_rows, width), jnp.float32),
            pltpu.VMEM((KVH, half_rows, 2 * HD), jnp.float32),
            pltpu.VMEM((KVH, half_rows, 2 * HD), jnp.float32),
            pltpu.SemaphoreType.DMA((micro_count, 2)),
            pltpu.SemaphoreType.DMA((micro_count, 2)),
            pltpu.SemaphoreType.DMA,
        ],
        compiler_params=pltpu.CompilerParams(
            collective_id=0, has_side_effects=True, vmem_limit_bytes=52 * 2**20
        ),
        cost_estimate=pl.CostEstimate(
            flops=2 * micro_count * length * width * (qkv_width + qd),
            bytes_accessed=24 * 2**20,
            transcendentals=0,
        ),
    )(cotangent, out_full, in_full, probs, keys, values, queries, inputs, scale, gain, table)


def with_swapped(rows):
    half_size = HD // 2
    swapped = jnp.concatenate([rows[..., half_size:], rows[..., :half_size]], axis=-1)
    return jnp.concatenate([rows, swapped], axis=-1)


def reduce_kernel(
    normed_ref,
    qkv_ref,
    upstream_ref,
    attn_ref,
    out_ref,
    for_twin,
    from_twin,
    stage,
    line,
    other,
    twin_send,
    twin_recv,
    line_send,
    line_recv,
    other_recv,
):
    mine = lax.axis_index("fsdp")
    place = mine // 2
    core = mine % 2
    places, shard, columns_out = stage.shape
    qkv_width = qkv_ref.shape[1]
    twin = place * 2 + 1 - core
    lower = lax.rem(place + places - 1, places) * 2 + core
    upper = lax.rem(place + 1, places) * 2 + core
    has_lower = place > 0
    has_upper = place < places - 1
    mesh_id = pl.DeviceIdType.MESH

    barrier = pltpu.get_barrier_semaphore()
    pl.semaphore_signal(barrier, inc=1, device_id={"fsdp": twin}, device_id_type=mesh_id)

    @pl.when(has_lower)
    def _():
        pl.semaphore_signal(barrier, inc=1, device_id={"fsdp": lower}, device_id_type=mesh_id)

    @pl.when(has_upper)
    def _():
        pl.semaphore_signal(barrier, inc=1, device_id={"fsdp": upper}, device_id_type=mesh_id)

    @pl.when(jnp.logical_and(has_lower, has_upper))
    def _():
        pl.semaphore_wait(barrier, 3)

    @pl.when(jnp.logical_not(jnp.logical_and(has_lower, has_upper)))
    def _():
        pl.semaphore_wait(barrier, 2)

    def remote(source, target, send, recv, device):
        return pltpu.make_async_remote_copy(
            src_ref=source,
            dst_ref=target,
            send_sem=send,
            recv_sem=recv,
            device_id={"fsdp": device},
            device_id_type=mesh_id,
        )

    def to_twin(t):
        return remote(for_twin.at[t], from_twin.at[t], twin_send.at[t], twin_recv.at[t], twin)

    def go_up(t):
        return remote(stage.at[t], line.at[t], line_send.at[t], line_recv.at[t], upper)

    def go_down(t):
        return remote(stage.at[t], line.at[t], line_send.at[t], line_recv.at[t], lower)

    def end_down(t):
        return remote(stage.at[t], other, line_send.at[t], other_recv, lower)

    across = (((0,), (0,)), ((), ()))

    def partial(t, which_core, store):
        rows = pl.ds(pl.multiple_of((t * 2 + which_core) * shard, shard), shard)

        def qkv_tile(tile, carry):
            columns = pl.ds(pl.multiple_of(tile * 512, 512), 512)
            store(
                columns,
                lax.dot_general(
                    normed_ref[:, rows],
                    qkv_ref[:, columns],
                    across,
                    preferred_element_type=jnp.float32,
                ),
            )
            return carry

        def out_tile(tile, carry):
            columns = pl.ds(pl.multiple_of(tile * 512, 512), 512)
            store(
                pl.ds(pl.multiple_of(qkv_width + tile * 512, 512), 512),
                lax.dot_general(
                    upstream_ref[:, rows],
                    attn_ref[:, columns],
                    across,
                    preferred_element_type=jnp.float32,
                ),
            )
            return carry

        lax.fori_loop(0, qkv_width // 512, qkv_tile, 0)
        lax.fori_loop(0, attn_ref.shape[1] // 512, out_tile, 0)

    low_half = place < places // 2

    def target(step):
        return jnp.where(low_half, places - 1 - step, step)

    def send_twin(step, carry):
        t = target(step)

        def store(columns, block):
            for_twin[t, :, columns] = block.astype(jnp.bfloat16)

        partial(t, 1 - core, store)
        to_twin(t).start()
        return carry

    lax.fori_loop(0, places, send_twin, 0)

    def chip_sum(step, carry):
        t = target(step)
        to_twin(t).wait_recv()

        def store(columns, block):
            stage[t, :, columns] = (
                block + from_twin[t, :, columns].astype(jnp.float32)
            ).astype(jnp.bfloat16)

        partial(t, core, store)

        @pl.when(jnp.logical_and(place == 0, t > place))
        def _():
            go_up(t).start()

        @pl.when(jnp.logical_and(place == places - 1, t < place - 1))
        def _():
            go_down(t).start()

        @pl.when(jnp.logical_and(place == places - 1, t == place - 1))
        def _():
            end_down(t).start()

        return carry

    lax.fori_loop(0, places, chip_sum, 0)

    def add_line(t):
        def tile(tile, carry):
            columns = pl.ds(pl.multiple_of(tile * 512, 512), 512)
            stage[t, :, columns] = (
                stage[t, :, columns].astype(jnp.float32) + line[t, :, columns].astype(jnp.float32)
            ).astype(jnp.bfloat16)
            return carry

        lax.fori_loop(0, columns_out // 512, tile, 0)

    def relay(tick, carry):
        @pl.when(jnp.logical_and(has_lower, place <= tick))
        def _():
            t = places - 1 - tick + place
            go_up(t).wait_recv()
            add_line(t)
            go_up(t).start()

        @pl.when(jnp.logical_and(has_upper, tick >= places - 1 - place))
        def _():
            t = tick - (places - 1 - place)
            go_down(t).wait_recv()
            add_line(t)

            @pl.when(t < place - 1)
            def _():
                go_down(t).start()

            @pl.when(t == place - 1)
            def _():
                end_down(t).start()

        return carry

    lax.fori_loop(0, places - 1, relay, 0)

    @pl.when(has_lower)
    def _():
        go_up(place).wait_recv()

    @pl.when(has_upper)
    def _():
        end_down(place).wait_recv()

    def finish(tile, carry):
        columns = pl.ds(pl.multiple_of(tile * 512, 512), 512)
        total = stage[place, :, columns].astype(jnp.float32)

        @pl.when(jnp.logical_not(has_lower))
        def _():
            out_ref[:, columns] = (total + other[:, columns].astype(jnp.float32)).astype(
                jnp.bfloat16
            )

        @pl.when(jnp.logical_not(has_upper))
        def _():
            out_ref[:, columns] = (total + line[place, :, columns].astype(jnp.float32)).astype(
                jnp.bfloat16
            )

        @pl.when(jnp.logical_and(has_lower, has_upper))
        def _():
            out_ref[:, columns] = (
                total
                + line[place, :, columns].astype(jnp.float32)
                + other[:, columns].astype(jnp.float32)
            ).astype(jnp.bfloat16)

        return carry

    lax.fori_loop(0, columns_out // 512, finish, 0)

    def sent(t, carry):
        to_twin(t).wait_send()

        @pl.when(t != place)
        def _():
            go_up(t).wait_send()

        return carry

    lax.fori_loop(0, places, sent, 0)


def weight_grads(normed, qkv, upstream, attn):
    tokens, width = normed.shape
    devices = lax.axis_size("fsdp")
    places = devices // 2
    shard = width // devices
    columns = qkv.shape[1] + attn.shape[1]
    vmem = pl.BlockSpec(memory_space=pltpu.VMEM)
    block = pltpu.VMEM((places, shard, columns), jnp.bfloat16)
    return pl.pallas_call(
        reduce_kernel,
        out_shape=jax.ShapeDtypeStruct((shard, columns), jnp.bfloat16),
        in_specs=[vmem] * 4,
        out_specs=vmem,
        scratch_shapes=[
            block,
            block,
            block,
            block,
            pltpu.VMEM((shard, columns), jnp.bfloat16),
            pltpu.SemaphoreType.DMA((places,)),
            pltpu.SemaphoreType.DMA((places,)),
            pltpu.SemaphoreType.DMA((places,)),
            pltpu.SemaphoreType.DMA((places,)),
            pltpu.SemaphoreType.DMA,
        ],
        compiler_params=pltpu.CompilerParams(
            collective_id=1, has_side_effects=True, vmem_limit_bytes=52 * 2**20
        ),
        cost_estimate=pl.CostEstimate(
            flops=2 * tokens * width * columns, bytes_accessed=8 * 2**20, transcendentals=0
        ),
    )(normed, qkv, upstream, attn)


def on_device(
    saved_inputs,
    saved_queries,
    saved_keys,
    saved_values,
    cotangent,
    norm_gain,
    query_weight,
    key_weight,
    value_weight,
    output_weight,
):
    inputs = saved_inputs[0]
    queries = saved_queries[0]
    keys_all = saved_keys[0]
    values_all = saved_values[0]
    gain_row = norm_gain[0]
    micro_count = inputs.shape[0]
    length = inputs.shape[1]
    width = inputs.shape[2]
    groups = HEADS // KVH
    out_full = lax.all_gather(output_weight[0], "fsdp", axis=0, tiled=True)
    in_shard = jnp.concatenate([query_weight[0], key_weight[0], value_weight[0]], axis=1)
    in_full = lax.all_gather(in_shard.T, "fsdp", axis=0, tiled=False)
    qkv_width = in_shard.shape[1]
    forward_all = jax.vmap(forward_parts, in_axes=(0, 0, 0, 0, None))
    attn_probs, normed, attn_out = forward_all(inputs, queries, keys_all, values_all, gain_row)
    scale_inv = norm_parts(inputs)[1]
    cosine, sine = rotary_tables(length, HD)
    table = jnp.concatenate([cosine, cosine, sine, -sine], axis=1)
    query_grid = with_swapped(
        queries.reshape(micro_count, length, KVH, groups, HD).transpose(0, 2, 3, 1, 4)
    )
    key_grid = with_swapped(keys_all.reshape(micro_count, length, KVH, HD).transpose(0, 2, 1, 3))
    value_grid = values_all.reshape(micro_count, length, KVH, HD).transpose(0, 2, 3, 1)
    value_grid = value_grid * jnp.bfloat16(1.0 / math.sqrt(HD))
    value_grid = jnp.concatenate([value_grid, value_grid], axis=2)
    grads, qkv_all, upstream_all = chain(
        cotangent,
        out_full,
        in_full,
        attn_probs,
        key_grid,
        value_grid,
        query_grid,
        inputs,
        scale_inv,
        norm_gain,
        table,
    )
    normed_flat = normed.reshape(micro_count * length, width)
    qkv_flat = qkv_all.reshape(micro_count * length, qkv_width)
    attn_flat = attn_out.reshape(micro_count * length, -1)
    upstream_flat = upstream_all.reshape(micro_count * length, width)
    summed = weight_grads(normed_flat, qkv_flat, upstream_flat, attn_flat)
    query_cols = query_weight.shape[2]
    key_cols = key_weight.shape[2]
    grad_query = summed[:, :query_cols]
    grad_key = summed[:, query_cols : query_cols + key_cols]
    grad_value = summed[:, query_cols + key_cols : qkv_width]
    grad_output = summed[:, qkv_width:]
    return (
        grads[None],
        grad_query[None],
        grad_key[None],
        grad_value[None],
        grad_output[None],
    )


def solution(mesh):
    return jax.shard_map(
        on_device,
        mesh=mesh,
        in_specs=(
            P("section", None, "fsdp", None),
            P("section", None, "fsdp", None),
            P("section", None, "fsdp", None),
            P("section", None, "fsdp", None),
            P(None, "fsdp", None),
            P("section", None),
            P("section", "fsdp", None),
            P("section", "fsdp", None),
            P("section", "fsdp", None),
            P("section", "fsdp", None),
        ),
        out_specs=(
            P("section", None, "fsdp", None),
            P("section", "fsdp", None),
            P("section", "fsdp", None),
            P("section", "fsdp", None),
            P("section", "fsdp", None),
        ),
        check_vma=False,
    )
```

```python
import math

import jax
import jax.numpy as jnp
from jax import lax
from jax.experimental import pallas as pl
from jax.experimental.pallas import tpu as pltpu
from jax.sharding import PartitionSpec as P

HEADS = 16
KVH = 4
HD = 64


norm_eps = 1e-05
rotary_base = 500000.0
masked_score = -1e30


def rotary_tables(length, head_size):
    half_size = head_size // 2
    inverse = jnp.exp(
        -(2.0 * jnp.arange(half_size, dtype=jnp.float32) / head_size) * math.log(rotary_base)
    )
    angles = jnp.arange(length, dtype=jnp.float32)[:, None] * inverse[None, :]
    return (jnp.cos(angles), jnp.sin(angles))


def chain_kernel(
    cotangent_ref,
    out_shard_ref,
    in_shard_ref,
    saved_queries_ref,
    saved_keys_ref,
    saved_values_ref,
    inputs_ref,
    gain_ref,
    table_ref,
    grad_ref,
    qkv_ref,
    normed_ref,
    attn_ref,
    upstream_ref,
    out_full_ref,
    in_full_ref,
    probs_ref,
    keys_ref,
    values_ref,
    queries_ref,
    scale_ref,
    held,
    d_attn,
    scaled_rows,
    key_sums,
    value_sums,
    send_sem,
    recv_sem,
    local_sem,
    up_send,
    down_send,
    twin_send,
    line_recv,
    twin_recv,
):
    section = lax.axis_index("section")
    sections = lax.axis_size("section")
    is_last = section == sections - 1
    below = lax.rem(section + sections - 1, sections)
    above = lax.rem(section + 1, sections)
    micro_count, length, width = grad_ref.shape
    half_rows = length // 2
    shards = in_full_ref.shape[0]
    shard = in_full_ref.shape[2]
    groups = HEADS // KVH
    qd = HEADS * HD
    kvd = KVH * HD
    mesh_id = pl.DeviceIdType.MESH
    mine = lax.axis_index("fsdp")
    place = mine // 2
    core = mine % 2
    places = shards // 2
    twin = place * 2 + 1 - core
    lower = lax.rem(place + places - 1, places) * 2 + core
    upper = lax.rem(place + 1, places) * 2 + core
    has_lower = place > 0
    has_upper = place < places - 1

    barrier = pltpu.get_barrier_semaphore()
    pl.semaphore_signal(barrier, inc=1, device_id={"fsdp": twin}, device_id_type=mesh_id)

    @pl.when(has_lower)
    def _():
        pl.semaphore_signal(barrier, inc=1, device_id={"fsdp": lower}, device_id_type=mesh_id)

    @pl.when(has_upper)
    def _():
        pl.semaphore_signal(barrier, inc=1, device_id={"fsdp": upper}, device_id_type=mesh_id)

    @pl.when(section < sections - 1)
    def _():
        pl.semaphore_signal(barrier, inc=1, device_id={"section": above}, device_id_type=mesh_id)

    out_full_ref[mine] = out_shard_ref[...]
    in_full_ref[mine] = in_shard_ref[...]
    peers = (
        1
        + has_lower.astype(jnp.int32)
        + has_upper.astype(jnp.int32)
        + (section > 0).astype(jnp.int32)
    )
    pl.semaphore_wait(barrier, peers)

    full_refs = (out_full_ref, in_full_ref)

    def to_device(which, t, send, recv, device):
        slot = t * 2 + core
        return pltpu.make_async_remote_copy(
            src_ref=full_refs[which].at[slot],
            dst_ref=full_refs[which].at[slot],
            send_sem=send.at[which, t],
            recv_sem=recv.at[which, t],
            device_id={"fsdp": device},
            device_id_type=mesh_id,
        )

    def go_up(which, t):
        return to_device(which, t, up_send, line_recv, upper)

    def go_down(which, t):
        return to_device(which, t, down_send, line_recv, lower)

    def to_twin(which, t):
        return to_device(which, t, twin_send, twin_recv, twin)

    def from_twin(which, t):
        slot = t * 2 + 1 - core
        return pltpu.make_async_remote_copy(
            src_ref=full_refs[which].at[slot],
            dst_ref=full_refs[which].at[slot],
            send_sem=twin_send.at[which, t],
            recv_sem=twin_recv.at[which, t],
            device_id={"fsdp": twin},
            device_id_type=mesh_id,
        )

    def gather_first(which):
        @pl.when(has_upper)
        def _():
            go_up(which, place).start()

        @pl.when(has_lower)
        def _():
            go_down(which, place).start()

        to_twin(which, place).start()

    def gather_step(which, step):
        low = place - step
        high = place + step

        @pl.when(low >= 0)
        def _():
            go_up(which, low).wait_recv()

            @pl.when(has_upper)
            def _():
                go_up(which, low).start()

            to_twin(which, low).start()

        @pl.when(high < places)
        def _():
            go_down(which, high).wait_recv()

            @pl.when(has_lower)
            def _():
                go_down(which, high).start()

            to_twin(which, high).start()

    def gather_end(which):
        def one(t, carry):
            from_twin(which, t).wait_recv()
            return carry

        lax.fori_loop(0, places, one, 0)

    def gather_sent(which):
        def one(t, carry):
            to_twin(which, t).wait_send()

            @pl.when(jnp.logical_and(has_upper, t <= place))
            def _():
                go_up(which, t).wait_send()

            @pl.when(jnp.logical_and(has_lower, t >= place))
            def _():
                go_down(which, t).wait_send()

            return carry

        lax.fori_loop(0, places, one, 0)

    lanes = lax.broadcasted_iota(jnp.int32, (length, 2 * HD), 1)
    front_all = lanes < HD
    front_quarter = lax.rem(lanes, HD) < HD // 2
    causal = lax.broadcasted_iota(jnp.int32, (length, length), 0) >= lax.broadcasted_iota(
        jnp.int32, (length, length), 1
    )
    last_dims = (((1,), (1,)), ((), ()))

    def swapped(block):
        return jnp.where(
            front_quarter,
            pltpu.roll(block, 2 * HD - HD // 2, 1),
            pltpu.roll(block, HD // 2, 1),
        )

    def one_head(own, beside, odd):
        if odd:
            return jnp.where(front_all, pltpu.roll(own, HD, 1), beside)
        return jnp.where(front_all, own, pltpu.roll(beside, HD, 1))

    def forward(micro):
        def square_tile(tile, total):
            columns = pl.ds(pl.multiple_of(tile * 256, 256), 256)
            block = inputs_ref[micro, :, columns].astype(jnp.float32)
            return total + jnp.sum(block * block, axis=-1, keepdims=True)

        total = lax.fori_loop(
            0, width // 256, square_tile, jnp.zeros((length, 1), jnp.float32)
        )
        scale_ref[micro] = lax.rsqrt(total * (1.0 / width) + norm_eps)

        def unit_tile(tile, carry):
            columns = pl.ds(pl.multiple_of(tile * 256, 256), 256)
            unit = inputs_ref[micro, :, columns].astype(jnp.float32) * scale_ref[micro]
            normed_ref[micro, :, columns] = (
                unit * gain_ref[:, columns].astype(jnp.float32)
            ).astype(jnp.bfloat16)
            return carry

        lax.fori_loop(0, width // 256, unit_tile, 0)

        def head_pair(pair, carry):
            columns = pl.ds(pl.multiple_of(pair * 2 * HD, 2 * HD), 2 * HD)
            key_block = saved_keys_ref[micro, :, columns].astype(jnp.float32)
            key_swapped = swapped(key_block)
            value_block = saved_values_ref[micro, :, columns].astype(jnp.float32)
            for odd in range(2):
                head = pair * 2 + odd
                key_rows = one_head(key_block, key_swapped, odd)
                keys_ref[micro, head] = key_rows.astype(jnp.bfloat16)
                key_alone = jnp.where(front_all, key_rows, 0.0).astype(jnp.bfloat16)
                value_rows = one_head(value_block, value_block, odd).astype(jnp.bfloat16)
                values_ref[micro, head] = value_rows
                for i in range(groups // 2):
                    start = pl.multiple_of((head * groups + 2 * i) * HD, 2 * HD)
                    query_block = saved_queries_ref[micro, :, pl.ds(start, 2 * HD)].astype(
                        jnp.float32
                    )
                    query_swapped = swapped(query_block)
                    outs = []
                    for second in range(2):
                        query_rows = one_head(query_block, query_swapped, second).astype(
                            jnp.bfloat16
                        )
                        queries_ref[micro, head, 2 * i + second] = query_rows
                        scores = lax.dot_general(
                            query_rows, key_alone, last_dims, preferred_element_type=jnp.float32
                        ) * (1.0 / math.sqrt(HD))
                        scores = jnp.where(causal, scores, masked_score)
                        row_peak = jnp.max(scores, axis=-1, keepdims=True)
                        weights = jnp.exp(scores - row_peak)
                        probs = (weights / jnp.sum(weights, axis=-1, keepdims=True)).astype(
                            jnp.bfloat16
                        )
                        probs_ref[micro, head, 2 * i + second] = probs
                        outs.append(
                            jnp.dot(probs, value_rows, preferred_element_type=jnp.float32)
                        )
                    attn_ref[micro, :, pl.ds(start, 2 * HD)] = jnp.where(
                        front_all, outs[0], outs[1]
                    ).astype(jnp.bfloat16)
            return carry

        lax.fori_loop(0, KVH // 2, head_pair, 0)

    gather_first(0)

    @pl.when(is_last)
    def _():
        own = pltpu.make_async_copy(cotangent_ref, held, local_sem)
        own.start()
        own.wait()

    for step in range(1, places):
        if step <= micro_count:
            forward(step - 1)
        gather_step(0, step)
    for micro in range(max(places - 1, 0), micro_count):
        forward(micro)
    gather_first(1)
    gather_end(0)
    for step in range(1, places):
        gather_step(1, step)
    gather_end(1)

    def hop(micro, half):
        rows = pl.ds(half * half_rows, half_rows)
        return pltpu.make_async_remote_copy(
            src_ref=grad_ref.at[micro, rows],
            dst_ref=held.at[micro, rows],
            send_sem=send_sem.at[micro, half],
            recv_sem=recv_sem.at[micro, half],
            device_id={"section": below},
            device_id_type=pl.DeviceIdType.MESH,
        )

    front = lax.broadcasted_iota(jnp.int32, (half_rows, 2 * HD), 1) < HD
    front_ones = jnp.where(front, 1.0, 0.0).astype(jnp.bfloat16)
    back_ones = jnp.where(front, 0.0, 1.0).astype(jnp.bfloat16)

    def both_halves(block):
        return block + pltpu.roll(block, HD, 1)

    def one_micro(micro, carry):
        for half in (1, 0):
            rows = pl.ds(half * half_rows, half_rows)
            span = (half + 1) * half_rows

            @pl.when(section < sections - 1)
            def _():
                hop(micro, half).wait_recv()

            def attn_tile(tile, carry):
                columns = pl.ds(pl.multiple_of(tile * 256, 256), 256)
                d_attn[:, columns] = jnp.dot(
                    held[micro, rows, :],
                    out_full_ref[:, :, columns].reshape(width, 256),
                    preferred_element_type=jnp.float32,
                ).astype(jnp.bfloat16)
                return carry

            lax.fori_loop(0, qd // 256, attn_tile, 0)
            table = table_ref[rows, :]
            kept = []
            for head in range(KVH):
                pairs = [
                    d_attn[:, (head * groups + 2 * i) * HD : (head * groups + 2 * i + 2) * HD]
                    for i in range(groups // 2)
                ]
                d_rows = jnp.concatenate(
                    [pair * ones for pair in pairs for ones in (front_ones, back_ones)], axis=0
                )
                probs = probs_ref[micro, head, :, rows, :span].reshape(groups * half_rows, span)
                d_probs = lax.dot_general(
                    d_rows,
                    values_ref[micro, head, :span, :],
                    last_dims,
                    preferred_element_type=jnp.float32,
                )
                probs_f = probs.astype(jnp.float32)
                row_inner = jnp.sum(probs_f * d_probs, axis=-1, keepdims=True)
                d_scores = (probs_f * (d_probs - row_inner) * (1.0 / math.sqrt(HD))).astype(
                    jnp.bfloat16
                )
                d_query = jnp.dot(
                    d_scores, keys_ref[micro, head, :span, :], preferred_element_type=jnp.float32
                )
                turned = [
                    both_halves(d_query[g * half_rows : (g + 1) * half_rows] * table)
                    for g in range(groups)
                ]
                for i in range(groups // 2):
                    start = (head * groups + 2 * i) * HD
                    qkv_ref[micro, rows, start : start + 2 * HD] = jnp.where(
                        front, turned[2 * i], turned[2 * i + 1]
                    ).astype(jnp.bfloat16)
                query_rows = queries_ref[micro, head, :, rows, :].reshape(
                    groups * half_rows, 2 * HD
                )
                across = (((0,), (0,)), ((), ()))
                d_key = lax.dot_general(
                    d_scores, query_rows, across, preferred_element_type=jnp.float32
                )
                d_value = lax.dot_general(
                    probs, d_rows, across, preferred_element_type=jnp.float32
                )
                if half == 1:
                    key_sums[head] = d_key[:half_rows]
                    value_sums[head] = d_value[:half_rows]
                    d_key = d_key[half_rows:]
                    d_value = d_value[half_rows:]
                else:
                    d_key = d_key + key_sums[head]
                    d_value = d_value + value_sums[head]
                kept.append((both_halves(d_key * table), both_halves(d_value)))
                if head % 2 == 1:
                    start = qd + (head - 1) * HD
                    for which in range(2):
                        at = start + which * kvd
                        qkv_ref[micro, rows, at : at + 2 * HD] = jnp.where(
                            front, kept[head - 1][which], kept[head][which]
                        ).astype(jnp.bfloat16)

            scale = scale_ref[micro, rows, :]

            def normed_tile(tile, inner):
                columns = pl.ds(pl.multiple_of(tile * shard, shard), shard)
                d_normed = jnp.dot(
                    qkv_ref[micro, rows, :], in_full_ref[tile], preferred_element_type=jnp.float32
                )
                scaled = d_normed * gain_ref[:, columns].astype(jnp.float32)
                scaled_rows[:, columns] = scaled
                unit = inputs_ref[micro, rows, columns].astype(jnp.float32) * scale
                return inner + jnp.sum(scaled * unit, axis=-1, keepdims=True)

            inner = lax.fori_loop(
                0, shards, normed_tile, jnp.zeros((half_rows, 1), jnp.float32)
            ) * (1.0 / width)

            def grad_tile(tile, carry):
                columns = pl.ds(pl.multiple_of(tile * shard, shard), shard)
                unit = inputs_ref[micro, rows, columns].astype(jnp.float32) * scale
                d_inputs = scale * (scaled_rows[:, columns] - unit * inner)
                grad_ref[micro, rows, columns] = (
                    held[micro, rows, columns].astype(jnp.float32) + d_inputs
                ).astype(jnp.bfloat16)
                return carry

            lax.fori_loop(0, shards, grad_tile, 0)

            @pl.when(section > 0)
            def _():
                hop(micro, half).start()

        return carry

    lax.fori_loop(0, micro_count, one_micro, 0)
    gather_sent(0)
    gather_sent(1)
    keep = pltpu.make_async_copy(held, upstream_ref, local_sem)
    keep.start()
    keep.wait()

    @pl.when(section > 0)
    def _():
        for micro in range(micro_count):
            for half in (1, 0):
                hop(micro, half).wait_send()


def chain(cotangent, out_shard, in_shard, queries, keys, values, inputs, gain, table):
    micro_count, length, width = inputs.shape
    half_rows = length // 2
    qd = HEADS * HD
    groups = HEADS // KVH
    qkv_width, shard = in_shard.shape
    shards = width // shard
    places = shards // 2
    vmem = pl.BlockSpec(memory_space=pltpu.VMEM)
    hbm = pl.BlockSpec(memory_space=pl.ANY)
    head_rows = pltpu.VMEM((micro_count, KVH, length, 2 * HD), jnp.bfloat16)
    sums = pltpu.VMEM((KVH, half_rows, 2 * HD), jnp.float32)
    gather_sem = pltpu.SemaphoreType.DMA((2, places))
    wide = jax.ShapeDtypeStruct((micro_count, length, width), jnp.bfloat16)
    return pl.pallas_call(
        chain_kernel,
        out_shape=(
            wide,
            jax.ShapeDtypeStruct((micro_count, length, qkv_width), jnp.bfloat16),
            wide,
            jax.ShapeDtypeStruct((micro_count, length, qd), jnp.bfloat16),
            wide,
        ),
        in_specs=[hbm] + [vmem] * 8,
        out_specs=(vmem, vmem, vmem, vmem, hbm),
        scratch_shapes=[
            pltpu.VMEM((shards, shard, qd), jnp.bfloat16),
            pltpu.VMEM((shards, qkv_width, shard), jnp.bfloat16),
            pltpu.VMEM((micro_count, KVH, groups, length, length), jnp.bfloat16),
            head_rows,
            head_rows,
            pltpu.VMEM((micro_count, KVH, groups, length, 2 * HD), jnp.bfloat16),
            pltpu.VMEM((micro_count, length, 1), jnp.float32),
            pltpu.VMEM((micro_count, length, width), jnp.bfloat16),
            pltpu.VMEM((half_rows, qd), jnp.bfloat16),
            pltpu.VMEM((half_rows, width), jnp.float32),
            sums,
            sums,
            pltpu.SemaphoreType.DMA((micro_count, 2)),
            pltpu.SemaphoreType.DMA((micro_count, 2)),
            pltpu.SemaphoreType.DMA,
            gather_sem,
            gather_sem,
            gather_sem,
            gather_sem,
            gather_sem,
        ],
        compiler_params=pltpu.CompilerParams(
            collective_id=0, has_side_effects=True, vmem_limit_bytes=56 * 2**20
        ),
        cost_estimate=pl.CostEstimate(
            flops=2 * micro_count * length * width * (qkv_width + qd),
            bytes_accessed=24 * 2**20,
            transcendentals=0,
        ),
    )(cotangent, out_shard, in_shard, queries, keys, values, inputs, gain, table)


def reduce_kernel(
    normed_ref,
    qkv_ref,
    upstream_ref,
    attn_ref,
    out_ref,
    for_twin,
    from_twin,
    stage,
    line,
    other,
    twin_send,
    twin_recv,
    line_send,
    line_recv,
    other_recv,
):
    mine = lax.axis_index("fsdp")
    place = mine // 2
    core = mine % 2
    places, shard, columns_out = stage.shape
    qkv_width = qkv_ref.shape[1]
    twin = place * 2 + 1 - core
    lower = lax.rem(place + places - 1, places) * 2 + core
    upper = lax.rem(place + 1, places) * 2 + core
    has_lower = place > 0
    has_upper = place < places - 1
    mesh_id = pl.DeviceIdType.MESH

    barrier = pltpu.get_barrier_semaphore()
    pl.semaphore_signal(barrier, inc=1, device_id={"fsdp": twin}, device_id_type=mesh_id)

    @pl.when(has_lower)
    def _():
        pl.semaphore_signal(barrier, inc=1, device_id={"fsdp": lower}, device_id_type=mesh_id)

    @pl.when(has_upper)
    def _():
        pl.semaphore_signal(barrier, inc=1, device_id={"fsdp": upper}, device_id_type=mesh_id)

    @pl.when(jnp.logical_and(has_lower, has_upper))
    def _():
        pl.semaphore_wait(barrier, 3)

    @pl.when(jnp.logical_not(jnp.logical_and(has_lower, has_upper)))
    def _():
        pl.semaphore_wait(barrier, 2)

    def remote(source, target, send, recv, device):
        return pltpu.make_async_remote_copy(
            src_ref=source,
            dst_ref=target,
            send_sem=send,
            recv_sem=recv,
            device_id={"fsdp": device},
            device_id_type=mesh_id,
        )

    def to_twin(t):
        return remote(for_twin.at[t], from_twin.at[t], twin_send.at[t], twin_recv.at[t], twin)

    def go_up(t):
        return remote(stage.at[t], line.at[t], line_send.at[t], line_recv.at[t], upper)

    def go_down(t):
        return remote(stage.at[t], line.at[t], line_send.at[t], line_recv.at[t], lower)

    def end_down(t):
        return remote(stage.at[t], other, line_send.at[t], other_recv, lower)

    across = (((0,), (0,)), ((), ()))

    def partial(t, which_core, store):
        rows = pl.ds(pl.multiple_of((t * 2 + which_core) * shard, shard), shard)

        def qkv_tile(tile, carry):
            columns = pl.ds(pl.multiple_of(tile * 512, 512), 512)
            store(
                columns,
                lax.dot_general(
                    normed_ref[:, rows],
                    qkv_ref[:, columns],
                    across,
                    preferred_element_type=jnp.float32,
                ),
            )
            return carry

        def out_tile(tile, carry):
            columns = pl.ds(pl.multiple_of(tile * 512, 512), 512)
            store(
                pl.ds(pl.multiple_of(qkv_width + tile * 512, 512), 512),
                lax.dot_general(
                    upstream_ref[:, rows],
                    attn_ref[:, columns],
                    across,
                    preferred_element_type=jnp.float32,
                ),
            )
            return carry

        lax.fori_loop(0, qkv_width // 512, qkv_tile, 0)
        lax.fori_loop(0, attn_ref.shape[1] // 512, out_tile, 0)

    low_half = place < places // 2

    def target(step):
        return jnp.where(low_half, places - 1 - step, step)

    def send_twin(step, carry):
        t = target(step)

        def store(columns, block):
            for_twin[t, :, columns] = block.astype(jnp.bfloat16)

        partial(t, 1 - core, store)
        to_twin(t).start()
        return carry

    lax.fori_loop(0, places, send_twin, 0)

    def chip_sum(step, carry):
        t = target(step)
        to_twin(t).wait_recv()

        def store(columns, block):
            stage[t, :, columns] = (
                block + from_twin[t, :, columns].astype(jnp.float32)
            ).astype(jnp.bfloat16)

        partial(t, core, store)

        @pl.when(jnp.logical_and(place == 0, t > place))
        def _():
            go_up(t).start()

        @pl.when(jnp.logical_and(place == places - 1, t < place - 1))
        def _():
            go_down(t).start()

        @pl.when(jnp.logical_and(place == places - 1, t == place - 1))
        def _():
            end_down(t).start()

        return carry

    lax.fori_loop(0, places, chip_sum, 0)

    def add_line(t):
        def tile(tile, carry):
            columns = pl.ds(pl.multiple_of(tile * 512, 512), 512)
            stage[t, :, columns] = (
                stage[t, :, columns].astype(jnp.float32) + line[t, :, columns].astype(jnp.float32)
            ).astype(jnp.bfloat16)
            return carry

        lax.fori_loop(0, columns_out // 512, tile, 0)

    def relay(tick, carry):
        @pl.when(jnp.logical_and(has_lower, place <= tick))
        def _():
            t = places - 1 - tick + place
            go_up(t).wait_recv()
            add_line(t)
            go_up(t).start()

        @pl.when(jnp.logical_and(has_upper, tick >= places - 1 - place))
        def _():
            t = tick - (places - 1 - place)
            go_down(t).wait_recv()
            add_line(t)

            @pl.when(t < place - 1)
            def _():
                go_down(t).start()

            @pl.when(t == place - 1)
            def _():
                end_down(t).start()

        return carry

    lax.fori_loop(0, places - 1, relay, 0)

    @pl.when(has_lower)
    def _():
        go_up(place).wait_recv()

    @pl.when(has_upper)
    def _():
        end_down(place).wait_recv()

    def finish(tile, carry):
        columns = pl.ds(pl.multiple_of(tile * 512, 512), 512)
        total = stage[place, :, columns].astype(jnp.float32)

        @pl.when(jnp.logical_not(has_lower))
        def _():
            out_ref[:, columns] = (total + other[:, columns].astype(jnp.float32)).astype(
                jnp.bfloat16
            )

        @pl.when(jnp.logical_not(has_upper))
        def _():
            out_ref[:, columns] = (total + line[place, :, columns].astype(jnp.float32)).astype(
                jnp.bfloat16
            )

        @pl.when(jnp.logical_and(has_lower, has_upper))
        def _():
            out_ref[:, columns] = (
                total
                + line[place, :, columns].astype(jnp.float32)
                + other[:, columns].astype(jnp.float32)
            ).astype(jnp.bfloat16)

        return carry

    lax.fori_loop(0, columns_out // 512, finish, 0)

    def sent(t, carry):
        to_twin(t).wait_send()

        @pl.when(t != place)
        def _():
            go_up(t).wait_send()

        return carry

    lax.fori_loop(0, places, sent, 0)


def weight_grads(normed, qkv, upstream, attn):
    tokens, width = normed.shape
    devices = lax.axis_size("fsdp")
    places = devices // 2
    shard = width // devices
    columns = qkv.shape[1] + attn.shape[1]
    vmem = pl.BlockSpec(memory_space=pltpu.VMEM)
    block = pltpu.VMEM((places, shard, columns), jnp.bfloat16)
    return pl.pallas_call(
        reduce_kernel,
        out_shape=jax.ShapeDtypeStruct((shard, columns), jnp.bfloat16),
        in_specs=[vmem] * 4,
        out_specs=vmem,
        scratch_shapes=[
            block,
            block,
            block,
            block,
            pltpu.VMEM((shard, columns), jnp.bfloat16),
            pltpu.SemaphoreType.DMA((places,)),
            pltpu.SemaphoreType.DMA((places,)),
            pltpu.SemaphoreType.DMA((places,)),
            pltpu.SemaphoreType.DMA((places,)),
            pltpu.SemaphoreType.DMA,
        ],
        compiler_params=pltpu.CompilerParams(
            collective_id=1, has_side_effects=True, vmem_limit_bytes=52 * 2**20
        ),
        cost_estimate=pl.CostEstimate(
            flops=2 * tokens * width * columns, bytes_accessed=8 * 2**20, transcendentals=0
        ),
    )(normed, qkv, upstream, attn)


def on_device(
    saved_inputs,
    saved_queries,
    saved_keys,
    saved_values,
    cotangent,
    norm_gain,
    query_weight,
    key_weight,
    value_weight,
    output_weight,
):
    inputs = saved_inputs[0]
    queries = saved_queries[0]
    keys_all = saved_keys[0]
    values_all = saved_values[0]
    micro_count = inputs.shape[0]
    length = inputs.shape[1]
    width = inputs.shape[2]
    in_shard = jnp.concatenate([query_weight[0], key_weight[0], value_weight[0]], axis=1)
    qkv_width = in_shard.shape[1]
    cosine, sine = rotary_tables(length, HD)
    table = jnp.concatenate([cosine, cosine, sine, -sine], axis=1)
    grads, qkv_all, normed, attn_out, upstream_all = chain(
        cotangent,
        output_weight[0],
        in_shard.T,
        queries,
        keys_all,
        values_all,
        inputs,
        norm_gain,
        table,
    )
    normed_flat = normed.reshape(micro_count * length, width)
    qkv_flat = qkv_all.reshape(micro_count * length, qkv_width)
    attn_flat = attn_out.reshape(micro_count * length, -1)
    upstream_flat = upstream_all.reshape(micro_count * length, width)
    summed = weight_grads(normed_flat, qkv_flat, upstream_flat, attn_flat)
    query_cols = query_weight.shape[2]
    key_cols = key_weight.shape[2]
    grad_query = summed[:, :query_cols]
    grad_key = summed[:, query_cols : query_cols + key_cols]
    grad_value = summed[:, query_cols + key_cols : qkv_width]
    grad_output = summed[:, qkv_width:]
    return (
        grads[None],
        grad_query[None],
        grad_key[None],
        grad_value[None],
        grad_output[None],
    )


def solution(mesh):
    return jax.shard_map(
        on_device,
        mesh=mesh,
        in_specs=(
            P("section", None, "fsdp", None),
            P("section", None, "fsdp", None),
            P("section", None, "fsdp", None),
            P("section", None, "fsdp", None),
            P(None, "fsdp", None),
            P("section", None),
            P("section", "fsdp", None),
            P("section", "fsdp", None),
            P("section", "fsdp", None),
            P("section", "fsdp", None),
        ),
        out_specs=(
            P("section", None, "fsdp", None),
            P("section", "fsdp", None),
            P("section", "fsdp", None),
            P("section", "fsdp", None),
            P("section", "fsdp", None),
        ),
        check_vma=False,
    )
```

```python
import math

import jax
import jax.numpy as jnp
from jax import lax
from jax.experimental import pallas as pl
from jax.experimental.pallas import tpu as pltpu
from jax.sharding import PartitionSpec as P

HEADS = 16
KVH = 4
HD = 64


norm_eps = 1e-05
rotary_base = 500000.0
masked_score = -1e30


def rotary_tables(length, head_size):
    half_size = head_size // 2
    inverse = jnp.exp(
        -(2.0 * jnp.arange(half_size, dtype=jnp.float32) / head_size) * math.log(rotary_base)
    )
    angles = jnp.arange(length, dtype=jnp.float32)[:, None] * inverse[None, :]
    return (jnp.cos(angles), jnp.sin(angles))


def chain_kernel(
    cotangent_ref,
    out_shard_ref,
    in_shard_ref,
    saved_queries_ref,
    saved_keys_ref,
    saved_values_ref,
    inputs_ref,
    gain_ref,
    table_ref,
    grad_ref,
    qkv_ref,
    normed_ref,
    attn_ref,
    upstream_ref,
    out_full_ref,
    in_full_ref,
    probs_ref,
    keys_ref,
    values_ref,
    queries_ref,
    scale_ref,
    held,
    d_attn,
    scaled_rows,
    key_sums,
    value_sums,
    send_sem,
    recv_sem,
    local_sem,
    up_send,
    down_send,
    twin_send,
    line_recv,
    twin_recv,
):
    section = lax.axis_index("section")
    sections = lax.axis_size("section")
    is_last = section == sections - 1
    below = lax.rem(section + sections - 1, sections)
    above = lax.rem(section + 1, sections)
    micro_count, length, width = grad_ref.shape
    half_rows = length // 2
    shards = in_full_ref.shape[0]
    shard = in_full_ref.shape[2]
    groups = HEADS // KVH
    qd = HEADS * HD
    kvd = KVH * HD
    mesh_id = pl.DeviceIdType.MESH
    mine = lax.axis_index("fsdp")
    place = mine // 2
    core = mine % 2
    places = shards // 2
    twin = place * 2 + 1 - core
    lower = lax.rem(place + places - 1, places) * 2 + core
    upper = lax.rem(place + 1, places) * 2 + core
    has_lower = place > 0
    has_upper = place < places - 1

    barrier = pltpu.get_barrier_semaphore()
    pl.semaphore_signal(barrier, inc=1, device_id={"fsdp": twin}, device_id_type=mesh_id)

    @pl.when(has_lower)
    def _():
        pl.semaphore_signal(barrier, inc=1, device_id={"fsdp": lower}, device_id_type=mesh_id)

    @pl.when(has_upper)
    def _():
        pl.semaphore_signal(barrier, inc=1, device_id={"fsdp": upper}, device_id_type=mesh_id)

    @pl.when(section < sections - 1)
    def _():
        pl.semaphore_signal(barrier, inc=1, device_id={"section": above}, device_id_type=mesh_id)

    out_full_ref[mine] = out_shard_ref[...]
    in_full_ref[mine] = in_shard_ref[...]
    peers = (
        1
        + has_lower.astype(jnp.int32)
        + has_upper.astype(jnp.int32)
        + (section > 0).astype(jnp.int32)
    )
    pl.semaphore_wait(barrier, peers)

    full_refs = (out_full_ref, in_full_ref)

    def to_device(which, t, send, recv, device):
        slot = t * 2 + core
        return pltpu.make_async_remote_copy(
            src_ref=full_refs[which].at[slot],
            dst_ref=full_refs[which].at[slot],
            send_sem=send.at[which, t],
            recv_sem=recv.at[which, t],
            device_id={"fsdp": device},
            device_id_type=mesh_id,
        )

    def go_up(which, t):
        return to_device(which, t, up_send, line_recv, upper)

    def go_down(which, t):
        return to_device(which, t, down_send, line_recv, lower)

    def to_twin(which, t):
        return to_device(which, t, twin_send, twin_recv, twin)

    def from_twin(which, t):
        slot = t * 2 + 1 - core
        return pltpu.make_async_remote_copy(
            src_ref=full_refs[which].at[slot],
            dst_ref=full_refs[which].at[slot],
            send_sem=twin_send.at[which, t],
            recv_sem=twin_recv.at[which, t],
            device_id={"fsdp": twin},
            device_id_type=mesh_id,
        )

    def gather_first(which):
        @pl.when(has_upper)
        def _():
            go_up(which, place).start()

        @pl.when(has_lower)
        def _():
            go_down(which, place).start()

        to_twin(which, place).start()

    def gather_step(which, step):
        low = place - step
        high = place + step

        @pl.when(low >= 0)
        def _():
            go_up(which, low).wait_recv()

            @pl.when(has_upper)
            def _():
                go_up(which, low).start()

            to_twin(which, low).start()

        @pl.when(high < places)
        def _():
            go_down(which, high).wait_recv()

            @pl.when(has_lower)
            def _():
                go_down(which, high).start()

            to_twin(which, high).start()

    def gather_end(which):
        def one(t, carry):
            from_twin(which, t).wait_recv()
            return carry

        lax.fori_loop(0, places, one, 0)

    def gather_sent(which):
        def one(t, carry):
            to_twin(which, t).wait_send()

            @pl.when(jnp.logical_and(has_upper, t <= place))
            def _():
                go_up(which, t).wait_send()

            @pl.when(jnp.logical_and(has_lower, t >= place))
            def _():
                go_down(which, t).wait_send()

            return carry

        lax.fori_loop(0, places, one, 0)

    lanes = lax.broadcasted_iota(jnp.int32, (length, 2 * HD), 1)
    front_all = lanes < HD
    front_quarter = lax.rem(lanes, HD) < HD // 2
    causal = lax.broadcasted_iota(jnp.int32, (length, length), 0) >= lax.broadcasted_iota(
        jnp.int32, (length, length), 1
    )
    last_dims = (((1,), (1,)), ((), ()))

    def swapped(block):
        return jnp.where(
            front_quarter,
            pltpu.roll(block, 2 * HD - HD // 2, 1),
            pltpu.roll(block, HD // 2, 1),
        )

    def one_head(own, beside, odd):
        if odd:
            return jnp.where(front_all, pltpu.roll(own, HD, 1), beside)
        return jnp.where(front_all, own, pltpu.roll(beside, HD, 1))

    def forward(micro):
        def square_tile(tile, total):
            columns = pl.ds(pl.multiple_of(tile * 256, 256), 256)
            block = inputs_ref[micro, :, columns].astype(jnp.float32)
            return total + jnp.sum(block * block, axis=-1, keepdims=True)

        total = lax.fori_loop(
            0, width // 256, square_tile, jnp.zeros((length, 1), jnp.float32)
        )
        scale_ref[micro] = lax.rsqrt(total * (1.0 / width) + norm_eps)

        def unit_tile(tile, carry):
            columns = pl.ds(pl.multiple_of(tile * 256, 256), 256)
            unit = inputs_ref[micro, :, columns].astype(jnp.float32) * scale_ref[micro]
            normed_ref[micro, :, columns] = (
                unit * gain_ref[:, columns].astype(jnp.float32)
            ).astype(jnp.bfloat16)
            return carry

        lax.fori_loop(0, width // 256, unit_tile, 0)

        def head_pair(pair, carry):
            columns = pl.ds(pl.multiple_of(pair * 2 * HD, 2 * HD), 2 * HD)
            key_block = saved_keys_ref[micro, :, columns].astype(jnp.float32)
            key_swapped = swapped(key_block)
            value_block = saved_values_ref[micro, :, columns].astype(jnp.float32)
            for odd in range(2):
                head = pair * 2 + odd
                key_rows = one_head(key_block, key_swapped, odd)
                keys_ref[micro, head] = key_rows.astype(jnp.bfloat16)
                key_alone = jnp.where(front_all, key_rows, 0.0).astype(jnp.bfloat16)
                value_rows = one_head(value_block, value_block, odd).astype(jnp.bfloat16)
                values_ref[micro, head] = value_rows
                for i in range(groups // 2):
                    start = pl.multiple_of((head * groups + 2 * i) * HD, 2 * HD)
                    query_block = saved_queries_ref[micro, :, pl.ds(start, 2 * HD)].astype(
                        jnp.float32
                    )
                    query_swapped = swapped(query_block)
                    outs = []
                    for second in range(2):
                        query_rows = one_head(query_block, query_swapped, second).astype(
                            jnp.bfloat16
                        )
                        queries_ref[micro, head, 2 * i + second] = query_rows
                        scores = lax.dot_general(
                            query_rows, key_alone, last_dims, preferred_element_type=jnp.float32
                        ) * (1.0 / math.sqrt(HD))
                        scores = jnp.where(causal, scores, masked_score)
                        row_peak = jnp.max(scores, axis=-1, keepdims=True)
                        weights = jnp.exp(scores - row_peak)
                        probs = (weights / jnp.sum(weights, axis=-1, keepdims=True)).astype(
                            jnp.bfloat16
                        )
                        probs_ref[micro, head, 2 * i + second] = probs
                        outs.append(
                            jnp.dot(probs, value_rows, preferred_element_type=jnp.float32)
                        )
                    attn_ref[micro, :, pl.ds(start, 2 * HD)] = jnp.where(
                        front_all, outs[0], outs[1]
                    ).astype(jnp.bfloat16)
            return carry

        lax.fori_loop(0, KVH // 2, head_pair, 0)

    def hop(micro, half):
        rows = pl.ds(half * half_rows, half_rows)
        return pltpu.make_async_remote_copy(
            src_ref=grad_ref.at[micro, rows],
            dst_ref=held.at[micro, rows],
            send_sem=send_sem.at[micro, half],
            recv_sem=recv_sem.at[micro, half],
            device_id={"section": below},
            device_id_type=pl.DeviceIdType.MESH,
        )

    front = lax.broadcasted_iota(jnp.int32, (half_rows, 2 * HD), 1) < HD
    front_ones = jnp.where(front, 1.0, 0.0).astype(jnp.bfloat16)
    back_ones = jnp.where(front, 0.0, 1.0).astype(jnp.bfloat16)

    def both_halves(block):
        return block + pltpu.roll(block, HD, 1)

    def attend(micro, half):
        rows = pl.ds(half * half_rows, half_rows)
        span = (half + 1) * half_rows

        def attn_tile(tile, carry):
            columns = pl.ds(pl.multiple_of(tile * 256, 256), 256)
            d_attn[:, columns] = jnp.dot(
                held[micro, rows, :],
                out_full_ref[:, :, columns].reshape(width, 256),
                preferred_element_type=jnp.float32,
            ).astype(jnp.bfloat16)
            return carry

        lax.fori_loop(0, qd // 256, attn_tile, 0)
        table = table_ref[rows, :]
        kept = []
        for head in range(KVH):
            pairs = [
                d_attn[:, (head * groups + 2 * i) * HD : (head * groups + 2 * i + 2) * HD]
                for i in range(groups // 2)
            ]
            d_rows = jnp.concatenate(
                [pair * ones for pair in pairs for ones in (front_ones, back_ones)], axis=0
            )
            probs = probs_ref[micro, head, :, rows, :span].reshape(groups * half_rows, span)
            d_probs = lax.dot_general(
                d_rows,
                values_ref[micro, head, :span, :],
                last_dims,
                preferred_element_type=jnp.float32,
            )
            probs_f = probs.astype(jnp.float32)
            row_inner = jnp.sum(probs_f * d_probs, axis=-1, keepdims=True)
            d_scores = (probs_f * (d_probs - row_inner) * (1.0 / math.sqrt(HD))).astype(
                jnp.bfloat16
            )
            d_query = jnp.dot(
                d_scores, keys_ref[micro, head, :span, :], preferred_element_type=jnp.float32
            )
            turned = [
                both_halves(d_query[g * half_rows : (g + 1) * half_rows] * table)
                for g in range(groups)
            ]
            for i in range(groups // 2):
                start = (head * groups + 2 * i) * HD
                qkv_ref[micro, rows, start : start + 2 * HD] = jnp.where(
                    front, turned[2 * i], turned[2 * i + 1]
                ).astype(jnp.bfloat16)
            query_rows = queries_ref[micro, head, :, rows, :].reshape(
                groups * half_rows, 2 * HD
            )
            across = (((0,), (0,)), ((), ()))
            d_key = lax.dot_general(
                d_scores, query_rows, across, preferred_element_type=jnp.float32
            )
            d_value = lax.dot_general(
                probs, d_rows, across, preferred_element_type=jnp.float32
            )
            if half == 1:
                key_sums[head] = d_key[:half_rows]
                value_sums[head] = d_value[:half_rows]
                d_key = d_key[half_rows:]
                d_value = d_value[half_rows:]
            else:
                d_key = d_key + key_sums[head]
                d_value = d_value + value_sums[head]
            kept.append((both_halves(d_key * table), both_halves(d_value)))
            if head % 2 == 1:
                start = qd + (head - 1) * HD
                for which in range(2):
                    at = start + which * kvd
                    qkv_ref[micro, rows, at : at + 2 * HD] = jnp.where(
                        front, kept[head - 1][which], kept[head][which]
                    ).astype(jnp.bfloat16)

    def project(micro, half):
        rows = pl.ds(half * half_rows, half_rows)
        scale = scale_ref[micro, rows, :]

        def normed_tile(tile, inner):
            columns = pl.ds(pl.multiple_of(tile * shard, shard), shard)
            d_normed = jnp.dot(
                qkv_ref[micro, rows, :], in_full_ref[tile], preferred_element_type=jnp.float32
            )
            scaled = d_normed * gain_ref[:, columns].astype(jnp.float32)
            scaled_rows[:, columns] = scaled
            unit = inputs_ref[micro, rows, columns].astype(jnp.float32) * scale
            return inner + jnp.sum(scaled * unit, axis=-1, keepdims=True)

        inner = lax.fori_loop(
            0, shards, normed_tile, jnp.zeros((half_rows, 1), jnp.float32)
        ) * (1.0 / width)

        def grad_tile(tile, carry):
            columns = pl.ds(pl.multiple_of(tile * shard, shard), shard)
            unit = inputs_ref[micro, rows, columns].astype(jnp.float32) * scale
            d_inputs = scale * (scaled_rows[:, columns] - unit * inner)
            grad_ref[micro, rows, columns] = (
                held[micro, rows, columns].astype(jnp.float32) + d_inputs
            ).astype(jnp.bfloat16)
            return carry

        lax.fori_loop(0, shards, grad_tile, 0)

        @pl.when(section > 0)
        def _():
            hop(micro, half).start()

    gather_first(0)

    @pl.when(is_last)
    def _():
        own = pltpu.make_async_copy(cotangent_ref, held, local_sem)
        own.start()
        own.wait()

    for step in range(1, places):
        if step <= micro_count:
            forward(step - 1)
        gather_step(0, step)
    for micro in range(max(places - 1, 0), micro_count):
        forward(micro)
    gather_first(1)
    gather_end(0)
    for step in range(1, places):
        if step <= micro_count:

            @pl.when(is_last)
            def _():
                attend(step - 1, 1)
                attend(step - 1, 0)

        gather_step(1, step)
    for micro in range(max(places - 1, 0), micro_count):

        @pl.when(is_last)
        def _():
            attend(micro, 1)
            attend(micro, 0)

    gather_end(1)

    def one_micro(micro, carry):
        for half in (1, 0):

            @pl.when(section < sections - 1)
            def _():
                hop(micro, half).wait_recv()
                attend(micro, half)

            project(micro, half)
        return carry

    lax.fori_loop(0, micro_count, one_micro, 0)
    gather_sent(0)
    gather_sent(1)
    keep = pltpu.make_async_copy(held, upstream_ref, local_sem)
    keep.start()
    keep.wait()

    @pl.when(section > 0)
    def _():
        for micro in range(micro_count):
            for half in (1, 0):
                hop(micro, half).wait_send()


def chain(cotangent, out_shard, in_shard, queries, keys, values, inputs, gain, table):
    micro_count, length, width = inputs.shape
    half_rows = length // 2
    qd = HEADS * HD
    groups = HEADS // KVH
    qkv_width, shard = in_shard.shape
    shards = width // shard
    places = shards // 2
    vmem = pl.BlockSpec(memory_space=pltpu.VMEM)
    hbm = pl.BlockSpec(memory_space=pl.ANY)
    head_rows = pltpu.VMEM((micro_count, KVH, length, 2 * HD), jnp.bfloat16)
    sums = pltpu.VMEM((KVH, half_rows, 2 * HD), jnp.float32)
    gather_sem = pltpu.SemaphoreType.DMA((2, places))
    wide = jax.ShapeDtypeStruct((micro_count, length, width), jnp.bfloat16)
    return pl.pallas_call(
        chain_kernel,
        out_shape=(
            wide,
            jax.ShapeDtypeStruct((micro_count, length, qkv_width), jnp.bfloat16),
            wide,
            jax.ShapeDtypeStruct((micro_count, length, qd), jnp.bfloat16),
            wide,
        ),
        in_specs=[hbm] + [vmem] * 8,
        out_specs=(vmem, vmem, vmem, vmem, hbm),
        scratch_shapes=[
            pltpu.VMEM((shards, shard, qd), jnp.bfloat16),
            pltpu.VMEM((shards, qkv_width, shard), jnp.bfloat16),
            pltpu.VMEM((micro_count, KVH, groups, length, length), jnp.bfloat16),
            head_rows,
            head_rows,
            pltpu.VMEM((micro_count, KVH, groups, length, 2 * HD), jnp.bfloat16),
            pltpu.VMEM((micro_count, length, 1), jnp.float32),
            pltpu.VMEM((micro_count, length, width), jnp.bfloat16),
            pltpu.VMEM((half_rows, qd), jnp.bfloat16),
            pltpu.VMEM((half_rows, width), jnp.float32),
            sums,
            sums,
            pltpu.SemaphoreType.DMA((micro_count, 2)),
            pltpu.SemaphoreType.DMA((micro_count, 2)),
            pltpu.SemaphoreType.DMA,
            gather_sem,
            gather_sem,
            gather_sem,
            gather_sem,
            gather_sem,
        ],
        compiler_params=pltpu.CompilerParams(
            collective_id=0, has_side_effects=True, vmem_limit_bytes=56 * 2**20
        ),
        cost_estimate=pl.CostEstimate(
            flops=2 * micro_count * length * width * (qkv_width + qd),
            bytes_accessed=24 * 2**20,
            transcendentals=0,
        ),
    )(cotangent, out_shard, in_shard, queries, keys, values, inputs, gain, table)


def reduce_kernel(
    normed_ref,
    qkv_ref,
    upstream_ref,
    attn_ref,
    query_out,
    key_out,
    value_out,
    output_out,
    for_twin,
    from_twin,
    stage,
    line,
    other,
    twin_send,
    twin_recv,
    line_send,
    line_recv,
    other_recv,
):
    mine = lax.axis_index("fsdp")
    place = mine // 2
    core = mine % 2
    places, shard, columns_out = stage.shape
    qkv_width = qkv_ref.shape[1]
    twin = place * 2 + 1 - core
    lower = lax.rem(place + places - 1, places) * 2 + core
    upper = lax.rem(place + 1, places) * 2 + core
    has_lower = place > 0
    has_upper = place < places - 1
    mesh_id = pl.DeviceIdType.MESH

    barrier = pltpu.get_barrier_semaphore()
    pl.semaphore_signal(barrier, inc=1, device_id={"fsdp": twin}, device_id_type=mesh_id)

    @pl.when(has_lower)
    def _():
        pl.semaphore_signal(barrier, inc=1, device_id={"fsdp": lower}, device_id_type=mesh_id)

    @pl.when(has_upper)
    def _():
        pl.semaphore_signal(barrier, inc=1, device_id={"fsdp": upper}, device_id_type=mesh_id)

    @pl.when(jnp.logical_and(has_lower, has_upper))
    def _():
        pl.semaphore_wait(barrier, 3)

    @pl.when(jnp.logical_not(jnp.logical_and(has_lower, has_upper)))
    def _():
        pl.semaphore_wait(barrier, 2)

    def remote(source, target, send, recv, device):
        return pltpu.make_async_remote_copy(
            src_ref=source,
            dst_ref=target,
            send_sem=send,
            recv_sem=recv,
            device_id={"fsdp": device},
            device_id_type=mesh_id,
        )

    def to_twin(t):
        return remote(for_twin.at[t], from_twin.at[t], twin_send.at[t], twin_recv.at[t], twin)

    part_columns = columns_out // 2

    def part_of(part):
        return pl.ds(part * part_columns, part_columns)

    def go(t, part, device):
        columns = part_of(part)
        return remote(
            stage.at[t, :, columns],
            line.at[t, :, columns],
            line_send.at[t, part],
            line_recv.at[t, part],
            device,
        )

    def go_up(t, part):
        return go(t, part, upper)

    def go_down(t, part):
        return go(t, part, lower)

    def end_down(t, part):
        columns = part_of(part)
        return remote(
            stage.at[t, :, columns],
            other.at[:, columns],
            line_send.at[t, part],
            other_recv.at[part],
            lower,
        )

    across = (((0,), (0,)), ((), ()))

    def partial(t, which_core, store):
        rows = pl.ds(pl.multiple_of((t * 2 + which_core) * shard, shard), shard)

        def qkv_tile(tile, carry):
            columns = pl.ds(pl.multiple_of(tile * 512, 512), 512)
            store(
                columns,
                lax.dot_general(
                    normed_ref[:, rows],
                    qkv_ref[:, columns],
                    across,
                    preferred_element_type=jnp.float32,
                ),
            )
            return carry

        def out_tile(tile, carry):
            columns = pl.ds(pl.multiple_of(tile * 512, 512), 512)
            store(
                pl.ds(pl.multiple_of(qkv_width + tile * 512, 512), 512),
                lax.dot_general(
                    upstream_ref[:, rows],
                    attn_ref[:, columns],
                    across,
                    preferred_element_type=jnp.float32,
                ),
            )
            return carry

        lax.fori_loop(0, qkv_width // 512, qkv_tile, 0)
        lax.fori_loop(0, attn_ref.shape[1] // 512, out_tile, 0)

    low_half = place < places // 2

    def target(step):
        return jnp.where(low_half, places - 1 - step, step)

    def send_twin(step):
        t = target(step)

        def store(columns, block):
            for_twin[t, :, columns] = block.astype(jnp.bfloat16)

        partial(t, 1 - core, store)
        to_twin(t).start()

    send_twin(0)

    def chip_sum(step, carry):
        @pl.when(step + 1 < places)
        def _():
            send_twin(step + 1)

        t = target(step)
        to_twin(t).wait_recv()

        def store(columns, block):
            stage[t, :, columns] = (
                block + from_twin[t, :, columns].astype(jnp.float32)
            ).astype(jnp.bfloat16)

        partial(t, core, store)

        @pl.when(jnp.logical_and(place == 0, t > place))
        def _():
            go_up(t, 0).start()
            go_up(t, 1).start()

        @pl.when(jnp.logical_and(place == places - 1, t < place - 1))
        def _():
            go_down(t, 0).start()
            go_down(t, 1).start()

        @pl.when(jnp.logical_and(place == places - 1, t == place - 1))
        def _():
            end_down(t, 0).start()
            end_down(t, 1).start()

        return carry

    lax.fori_loop(0, places, chip_sum, 0)

    def add_line(t, part):
        def tile(tile, carry):
            columns = pl.ds(
                pl.multiple_of(part * part_columns + tile * 256, 256), 256
            )
            stage[t, :, columns] = (
                stage[t, :, columns].astype(jnp.float32) + line[t, :, columns].astype(jnp.float32)
            ).astype(jnp.bfloat16)
            return carry

        lax.fori_loop(0, part_columns // 256, tile, 0)

    def relay(tick, carry):
        for part in range(2):

            @pl.when(jnp.logical_and(has_lower, place <= tick))
            def _():
                t = places - 1 - tick + place
                go_up(t, part).wait_recv()
                add_line(t, part)
                go_up(t, part).start()

            @pl.when(jnp.logical_and(has_upper, tick >= places - 1 - place))
            def _():
                t = tick - (places - 1 - place)
                go_down(t, part).wait_recv()
                add_line(t, part)

                @pl.when(t < place - 1)
                def _():
                    go_down(t, part).start()

                @pl.when(t == place - 1)
                def _():
                    end_down(t, part).start()

        return carry

    lax.fori_loop(0, places - 1, relay, 0)

    for part in range(2):

        @pl.when(has_lower)
        def _():
            go_up(place, part).wait_recv()

        @pl.when(has_upper)
        def _():
            end_down(place, part).wait_recv()

    def finish(out_ref, start):
        def tile(tile, carry):
            columns = pl.ds(pl.multiple_of(start + tile * 256, 256), 256)
            own_columns = pl.ds(pl.multiple_of(tile * 256, 256), 256)
            total = stage[place, :, columns].astype(jnp.float32)

            @pl.when(jnp.logical_not(has_lower))
            def _():
                out_ref[:, own_columns] = (
                    total + other[:, columns].astype(jnp.float32)
                ).astype(jnp.bfloat16)

            @pl.when(jnp.logical_not(has_upper))
            def _():
                out_ref[:, own_columns] = (
                    total + line[place, :, columns].astype(jnp.float32)
                ).astype(jnp.bfloat16)

            @pl.when(jnp.logical_and(has_lower, has_upper))
            def _():
                out_ref[:, own_columns] = (
                    total
                    + line[place, :, columns].astype(jnp.float32)
                    + other[:, columns].astype(jnp.float32)
                ).astype(jnp.bfloat16)

            return carry

        lax.fori_loop(0, out_ref.shape[1] // 256, tile, 0)

    start = 0
    for out_ref in (query_out, key_out, value_out, output_out):
        finish(out_ref, start)
        start += out_ref.shape[1]

    def sent(t, carry):
        to_twin(t).wait_send()

        @pl.when(t != place)
        def _():
            go_up(t, 0).wait_send()
            go_up(t, 1).wait_send()

        return carry

    lax.fori_loop(0, places, sent, 0)


def weight_grads(normed, qkv, upstream, attn):
    tokens, width = normed.shape
    devices = lax.axis_size("fsdp")
    places = devices // 2
    shard = width // devices
    columns = qkv.shape[1] + attn.shape[1]
    vmem = pl.BlockSpec(memory_space=pltpu.VMEM)
    block = pltpu.VMEM((places, shard, columns), jnp.bfloat16)
    return pl.pallas_call(
        reduce_kernel,
        out_shape=tuple(
            jax.ShapeDtypeStruct((shard, size), jnp.bfloat16)
            for size in (HEADS * HD, KVH * HD, KVH * HD, attn.shape[1])
        ),
        in_specs=[vmem] * 4,
        out_specs=(vmem,) * 4,
        scratch_shapes=[
            block,
            block,
            block,
            block,
            pltpu.VMEM((shard, columns), jnp.bfloat16),
            pltpu.SemaphoreType.DMA((places,)),
            pltpu.SemaphoreType.DMA((places,)),
            pltpu.SemaphoreType.DMA((places, 2)),
            pltpu.SemaphoreType.DMA((places, 2)),
            pltpu.SemaphoreType.DMA((2,)),
        ],
        compiler_params=pltpu.CompilerParams(
            collective_id=1, has_side_effects=True, vmem_limit_bytes=52 * 2**20
        ),
        cost_estimate=pl.CostEstimate(
            flops=2 * tokens * width * columns, bytes_accessed=8 * 2**20, transcendentals=0
        ),
    )(normed, qkv, upstream, attn)


def on_device(
    saved_inputs,
    saved_queries,
    saved_keys,
    saved_values,
    cotangent,
    norm_gain,
    query_weight,
    key_weight,
    value_weight,
    output_weight,
):
    inputs = saved_inputs[0]
    queries = saved_queries[0]
    keys_all = saved_keys[0]
    values_all = saved_values[0]
    micro_count = inputs.shape[0]
    length = inputs.shape[1]
    width = inputs.shape[2]
    in_shard = jnp.concatenate([query_weight[0], key_weight[0], value_weight[0]], axis=1)
    qkv_width = in_shard.shape[1]
    cosine, sine = rotary_tables(length, HD)
    table = jnp.concatenate([cosine, cosine, sine, -sine], axis=1)
    grads, qkv_all, normed, attn_out, upstream_all = chain(
        cotangent,
        output_weight[0],
        in_shard.T,
        queries,
        keys_all,
        values_all,
        inputs,
        norm_gain,
        table,
    )
    normed_flat = normed.reshape(micro_count * length, width)
    qkv_flat = qkv_all.reshape(micro_count * length, qkv_width)
    attn_flat = attn_out.reshape(micro_count * length, -1)
    upstream_flat = upstream_all.reshape(micro_count * length, width)
    grad_query, grad_key, grad_value, grad_output = weight_grads(
        normed_flat, qkv_flat, upstream_flat, attn_flat
    )
    return (
        grads[None],
        grad_query[None],
        grad_key[None],
        grad_value[None],
        grad_output[None],
    )


def solution(mesh):
    return jax.shard_map(
        on_device,
        mesh=mesh,
        in_specs=(
            P("section", None, "fsdp", None),
            P("section", None, "fsdp", None),
            P("section", None, "fsdp", None),
            P("section", None, "fsdp", None),
            P(None, "fsdp", None),
            P("section", None),
            P("section", "fsdp", None),
            P("section", "fsdp", None),
            P("section", "fsdp", None),
            P("section", "fsdp", None),
        ),
        out_specs=(
            P("section", None, "fsdp", None),
            P("section", "fsdp", None),
            P("section", "fsdp", None),
            P("section", "fsdp", None),
            P("section", "fsdp", None),
        ),
        check_vma=False,
    )
```
